32 devices in a mesh: ctx: 8 (over z, core), head: 4 (over y, x).
Axes of the slice: x: 2, y: 2, z: 4, core: 2. Of those that a mesh axis runs over, the one named last changes fastest.
Arguments:
- query_states: bfloat16 [16384, 16, 128], P('ctx', 'head'), may hold values from -36 to 36, as said below
- key_states: bfloat16 [16384, 16, 128], P('ctx', 'head'), may hold values from -6 to 6
- value_states: bfloat16 [16384, 16, 128], P('ctx', 'head'), may hold values from -6 to 6
- block_pattern: int32 [16, 128, 128], P('head'), may hold values 0 or 1
- helper_distances: int32 [2], replicated, may hold values from 1 to 4, as said below
- out_weight: bfloat16 [16, 128, 4096], P('head'), may hold values from -0.125 to 0.125
Outputs:
- layer_output: bfloat16 [16384, 4096], P(('ctx', 'head'))
The draws below stay inside these ranges and needn't reach their ends.
Inputs may be any that keep to these rules, and one draw needn't show every extreme that they name: `query_states`: Queries; some rows may be large multiples of key rows. `helper_distances`: the two distances differ, and one of them is always 8.
All inputs are finite; a program needn't handle non-finite values. No bound on the sum of `block_pattern` on one device may be relied on, other than what follows from the above.
Results may differ from the reference program's by a relative error of at most 0.015.
Values may be sent and summed in bfloat16 or wider, within the bound.
No kernel may reach another device: no remote copies, remote signals or barrier semaphores. Data moves between devices by JAX's collectives and lax.ppermute only.
A program may use at most 128 MiB of HBM per device.

```python
import jax
import jax.numpy as jnp
from jax import lax

D = 4096
HEADS = 16
HEAD_DIM = 128
BLOCK = 128
ROUNDS = 2
CTX_DEV = 2048
SHARDS = 8
SEQ = 16384
NB = 128
N_HEAD = 4


def draw_pair(key):
    full_shape = (SEQ, HEADS, HEAD_DIM)
    query_key = jax.random.fold_in(key, 7001)
    state_key = jax.random.fold_in(key, 7002)
    queries = jnp.clip(jax.random.normal(query_key, full_shape, jnp.float32), -6.0, 6.0)
    states = jnp.clip(jax.random.normal(state_key, full_shape, jnp.float32), -6.0, 6.0)
    return (queries, states)


def draw_query_states(key, part):
    return draw_pair(key)[0].astype(jnp.bfloat16)


def draw_key_states(key, part):
    return draw_pair(key)[1].astype(jnp.bfloat16)


def draw_helper_distances(key, part):
    half_way = SHARDS // 2
    other_hop = jax.random.randint(jax.random.fold_in(key, 9101), (), 1, half_way)
    flip_bit = jax.random.randint(jax.random.fold_in(key, 9102), (), 0, 2)
    first_hop = jnp.where(flip_bit == 1, half_way, other_hop)
    second_hop = jnp.where(flip_bit == 1, other_hop, half_way)
    return jnp.stack([first_hop, second_hop]).astype(jnp.int32)


def plant(drawn, rng, least, top_value):
    longest = drawn.shape.index(max(drawn.shape))
    spots = []
    for shift in (0, 1):
        where = [jax.random.randint(jax.random.fold_in(rng, axis), (), 0, length) for axis, length in enumerate(drawn.shape)]
        where[longest] = (where[longest] + shift) % drawn.shape[longest]
        spots.append(tuple(where))
    return drawn.at[spots[0]].set(least).at[spots[1]].set(top_value)


def levels(key, dims, cuts, smallest, largest):
    level, own = 1.0, jax.random.fold_in(key, 6)
    for position, blocks in cuts:
        heights = jnp.exp(jax.random.uniform(jax.random.fold_in(own, position), (blocks,), jnp.float32, smallest / len(cuts), largest / len(cuts)))
        level = level * jnp.repeat(heights, dims[position] // blocks).reshape([-1 if axis == position else 1 for axis in range(len(dims))])
    return level


def centred(rng, extent, scale, most, split=(), kind=jnp.bfloat16):
    values = jax.random.normal(rng, extent, jnp.float32) * scale
    if len(split) > 0:
        values = levels(rng, extent, split, -0.22, 0.18) * values
    return jnp.clip(values, min=-most, max=most).astype(kind)


def setup_inputs(seed: int = 0) -> dict:
    key_of = jax.random.split(jax.random.key(seed), 7)
    query_states = draw_query_states(jax.random.fold_in(key_of[6], 71), 0)
    key_states = draw_key_states(jax.random.fold_in(key_of[6], 71), 0)
    value_states = centred(key_of[2], (SEQ, HEADS, HEAD_DIM), 1.0, 6.0, ((0, 8), (1, 4)))
    block_pattern = plant((jax.random.randint(key_of[3], (HEADS, NB, NB), 0, 5) < 2).astype(jnp.int32), jax.random.fold_in(key_of[3], 1), 0, 1)
    helper_distances = draw_helper_distances(jax.random.fold_in(key_of[6], 71), 0)
    out_weight = centred(key_of[5], (HEADS, HEAD_DIM, D), (HEADS * HEAD_DIM) ** -0.5, 0.125, ((0, 4),))
    return {"query_states": query_states, "key_states": key_states, "value_states": value_states, "block_pattern": block_pattern, "helper_distances": helper_distances, "out_weight": out_weight}


NEG_FILL = -1.0e30


def attend_source(query_part, key_part, value_part, pattern_rows, is_local):
    row_count = query_part.shape[0]
    key_count = key_part.shape[0]
    row_step = min(512, row_count)
    score_scale = query_part.shape[2] ** -0.5
    key_place = jnp.arange(key_count, dtype=jnp.int32)

    def one_block(block_number):
        first_row = (block_number * row_step).astype(jnp.int32)
        query_rows = lax.dynamic_slice_in_dim(query_part, first_row, row_step, 0)
        pattern_part = lax.dynamic_slice_in_dim(pattern_rows, (first_row // BLOCK).astype(jnp.int32), row_step // BLOCK, 1)
        allowed = jnp.repeat(jnp.repeat(pattern_part > 0, BLOCK, axis=1), BLOCK, axis=2)
        if is_local:
            query_place = first_row + jnp.arange(row_step, dtype=jnp.int32)
            query_block = query_place // BLOCK
            key_block = key_place // BLOCK
            earlier = key_block[None, :] < query_block[:, None]
            same_block = (key_block[None, :] == query_block[:, None]) & (key_place[None, :] <= query_place[:, None])
            allowed = (allowed & earlier[None]) | same_block[None]
        scores = jnp.einsum("qhe,khe->hqk", query_rows.astype(jnp.float32), key_part.astype(jnp.float32),
                            precision=lax.Precision.HIGHEST) * score_scale
        masked = jnp.where(allowed, scores, NEG_FILL)
        row_peak = jnp.max(masked, axis=2)
        weights = jnp.where(allowed, jnp.exp(masked - row_peak[:, :, None]), 0.0)
        row_total = jnp.sum(weights, axis=2)
        rounded = lax.optimization_barrier(weights.astype(jnp.bfloat16)).astype(jnp.float32)
        numerator = jnp.einsum("hqk,khe->qhe", rounded, value_part.astype(jnp.float32),
                               precision=lax.Precision.HIGHEST)
        return numerator, row_peak.T, row_total.T

    numerator, row_peak, row_total = lax.map(one_block, jnp.arange(row_count // row_step, dtype=jnp.int32))
    heads_here = query_part.shape[1]
    return (numerator.reshape(row_count, heads_here, query_part.shape[2]),
            row_peak.reshape(row_count, heads_here), row_total.reshape(row_count, heads_here))


def keep_valid(piece, is_valid):
    numerator, row_peak, row_total = piece
    return (jnp.where(is_valid, numerator, 0.0), jnp.where(is_valid, row_peak, NEG_FILL),
            jnp.where(is_valid, row_total, 0.0))


def combine_sources(pieces):
    peak_score = pieces[0][1]
    for piece in pieces[1:]:
        peak_score = jnp.maximum(peak_score, piece[1])
    numerator_sum = jnp.zeros_like(pieces[0][0])
    denominator = jnp.zeros_like(pieces[0][1])
    for numerator, row_peak, row_total in pieces:
        factor = jnp.exp(row_peak - peak_score)
        numerator_sum = numerator_sum + factor[:, :, None] * numerator
        denominator = denominator + factor * row_total
    return (numerator_sum / denominator[:, :, None]).astype(jnp.bfloat16)


def reference(query_states, key_states, value_states, block_pattern, helper_distances, out_weight):
    per_shard = CTX_DEV // BLOCK

    def pattern_rows(query_shard, key_shard):
        starts = (jnp.zeros((), jnp.int32), (query_shard * per_shard).astype(jnp.int32),
                  (key_shard * per_shard).astype(jnp.int32))
        return lax.dynamic_slice(block_pattern, starts, (HEADS, per_shard, per_shard))

    def one_shard(my_shard):
        start_row = (my_shard * CTX_DEV).astype(jnp.int32)
        query_part = lax.dynamic_slice_in_dim(query_states, start_row, CTX_DEV, 0)
        key_part = lax.dynamic_slice_in_dim(key_states, start_row, CTX_DEV, 0)
        value_part = lax.dynamic_slice_in_dim(value_states, start_row, CTX_DEV, 0)
        pieces = [attend_source(query_part, key_part, value_part, pattern_rows(my_shard, my_shard), True)]
        for round_number in range(ROUNDS):
            source = my_shard - helper_distances[round_number].astype(jnp.int32)
            safe_source = jnp.maximum(source, 0).astype(jnp.int32)
            far_start = (safe_source * CTX_DEV).astype(jnp.int32)
            far_keys = lax.dynamic_slice_in_dim(key_states, far_start, CTX_DEV, 0)
            far_values = lax.dynamic_slice_in_dim(value_states, far_start, CTX_DEV, 0)
            piece = attend_source(query_part, far_keys, far_values, pattern_rows(my_shard, safe_source), False)
            pieces.append(keep_valid(piece, source >= 0))
        return combine_sources(pieces)

    attended = lax.map(one_shard, jnp.arange(SHARDS, dtype=jnp.int32))
    flattened = attended.reshape(SEQ, HEADS * HEAD_DIM)
    weight_rows = out_weight.reshape(HEADS * HEAD_DIM, D)
    group_width = (HEADS // N_HEAD) * HEAD_DIM
    output_sum = jnp.zeros((SEQ, D), jnp.float32)
    for group in range(N_HEAD):
        partial_value = jnp.dot(flattened[:, group * group_width:(group + 1) * group_width],
                          weight_rows[group * group_width:(group + 1) * group_width],
                          preferred_element_type=jnp.float32)
        partial_value = lax.optimization_barrier(partial_value.astype(jnp.bfloat16))
        output_sum = output_sum + partial_value.astype(jnp.float32)
    return output_sum.astype(jnp.bfloat16)
```

```python
import functools

import jax
import jax.numpy as jnp
from jax import lax
from jax.experimental import pallas as pl
from jax.experimental.pallas import tpu as pltpu
from jax.sharding import PartitionSpec as P

BLOCK = 128
LANES = 128
STAT_ROWS = 16
NEG_FILL = -1e30
LEAST_PEAK = -5e29
LOG2E = 1.4426950408889634
NT = (((1,), (1,)), ((), ()))
VMEM_BYTES = 60 * 2**20


def kernel_call(body, name, micros, **options):
    return pl.pallas_call(
        body,
        name=name,
        cost_estimate=pl.CostEstimate(flops=int(micros * 1.15e9), bytes_accessed=1, transcendentals=0),
        compiler_params=pltpu.CompilerParams(vmem_limit_bytes=VMEM_BYTES),
        **options,
    )


def helper_job(info_ref, number):
    me, distance = info_ref[0], info_ref[2 + number]
    odd = distance & 1
    hops = (distance + odd * (1 - 2 * (me & 1))) >> 1
    query_shard = me + 2 * hops
    return hops, query_shard, query_shard - distance, odd


def bias_rows(pattern_ref, query_shard, key_shard, blocks, is_local):
    count = pattern_ref.shape[1] // blocks
    query_shard = jnp.clip(query_shard, 0, count - 1)
    key_shard = jnp.clip(key_shard, 0, count - 1)
    rows = pattern_ref[0, pl.ds(pl.multiple_of(query_shard * blocks, blocks), blocks), :]
    width = rows.shape[1]
    rows = pltpu.roll(rows, width - key_shard * blocks, 1)
    if width >= LANES:
        rows = rows[:, :LANES]
    else:
        rows = jnp.concatenate([rows, jnp.zeros((blocks, LANES - width), rows.dtype)], 1)
    query_block = lax.broadcasted_iota(jnp.int32, rows.shape, 0)
    key_block = lax.broadcasted_iota(jnp.int32, rows.shape, 1)
    seen = rows > 0
    if is_local:
        seen = seen & (key_block < query_block) | (key_block == query_block)
    return jnp.where(seen | (key_block >= blocks), 0.0, NEG_FILL)


def mark_blocks(ref):
    block_of = lax.broadcasted_iota(jnp.int32, ref.shape, 0) // BLOCK
    lane = lax.broadcasted_iota(jnp.int32, ref.shape, 1)
    ref[...] = jnp.where(block_of == lane, 1.0, 0.0).astype(jnp.bfloat16)


def prepare_body(info_ref, value_ref, pattern_ref, turned_value_ref, local_ref, *bias_refs, spots):
    tokens = value_ref.shape[0]
    turned_value_ref[0, :LANES, :] = value_ref[...].T
    turned_value_ref[0, LANES:, :] = jnp.ones((STAT_ROWS, tokens), jnp.bfloat16)
    local_ref[0] = bias_rows(pattern_ref, info_ref[0], info_ref[0], len(spots), True)
    for number, out_ref in enumerate(bias_refs):
        _, query_shard, key_shard, _ = helper_job(info_ref, number)
        rows = bias_rows(pattern_ref, query_shard, key_shard, len(spots), False)
        for block, spot in enumerate(spots):
            out_ref[0, spot : spot + 1, :] = rows[block : block + 1, :]


def prepare(info, values, block_pattern, spots):
    tokens, width = values.shape
    heads = width // LANES
    out_shapes = [(LANES + STAT_ROWS, tokens)] + [(len(spots), LANES)] * 3
    out_types = [jnp.bfloat16] + [jnp.float32] * 3
    return kernel_call(
        functools.partial(prepare_body, spots=spots),
        "prepare",
        4,
        grid=(heads,),
        in_specs=[
            pl.BlockSpec(memory_space=pltpu.SMEM),
            pl.BlockSpec((tokens, LANES), lambda h: (0, h)),
            pl.BlockSpec((1, *block_pattern.shape[1:]), lambda h: (h, 0, 0)),
        ],
        out_specs=[pl.BlockSpec((1, *shape), lambda h: (h, 0, 0)) for shape in out_shapes],
        out_shape=[
            jax.ShapeDtypeStruct((heads, *shape), kind) for shape, kind in zip(out_shapes, out_types)
        ],
    )(info, values, block_pattern)


def widen_queries(queries, bias_rows):
    scaled = (queries.astype(jnp.float32) * (LANES**-0.5 * LOG2E)).astype(jnp.bfloat16)
    rows = queries.shape[0] // len(bias_rows)
    bias = [jnp.broadcast_to(row, (rows, LANES)).astype(jnp.bfloat16) for row in bias_rows]
    return jnp.concatenate([scaled, jnp.concatenate(bias, 0)], 1)


def split_three(value):
    high = value.astype(jnp.bfloat16).astype(jnp.float32)
    rest = value - high
    middle = rest.astype(jnp.bfloat16).astype(jnp.float32)
    low = rest - middle
    return jnp.concatenate([high, middle, low, jnp.zeros_like(low)], 0)


def peak_eight(scores):
    return jnp.max(scores.reshape(scores.shape[0] // 8, 8, scores.shape[1]), 0)


def finish_rows(numerator, peak):
    total = jnp.maximum(numerator[LANES : LANES + 1], 1e-30)
    normal = (numerator[:LANES] * (1.0 / total)).astype(jnp.bfloat16)
    return normal, split_three(peak + jnp.log2(total))


def far_body(info_ref, *refs, places, tile, step, first_block):
    sources = 2
    query_refs, refs = refs[:places], refs[places:]
    key_refs, value_refs, bias_refs, out_refs, joined_ref, refs = (
        refs[:2],
        refs[2:4],
        refs[4:6],
        refs[6:8],
        refs[8],
        refs[9:],
    )
    (
        held_queries,
        held_bias,
        held_keys,
        held_values,
        marks,
        held_out,
        score_a,
        score_b,
        query_sems,
        key_sems,
        value_sems,
        out_sems,
    ) = refs
    heads, _, tokens = value_refs[0].shape
    jobs = [helper_job(info_ref, number) for number in range(sources)]
    rows = query_refs[0].shape[0]
    tiles = sources * rows // tile
    per_tile = tile // BLOCK
    per_source = rows // tile
    scores = (score_a, score_b)

    def query_copy(source, place):
        target = held_queries.at[source * rows : (source + 1) * rows, :]
        return pltpu.make_async_copy(query_refs[place], target, query_sems.at[source])

    def key_copy(source, head, owner):
        lanes = pl.ds(pl.multiple_of(head * LANES, LANES), LANES)
        return pltpu.make_async_copy(
            key_refs[owner].at[:, lanes], held_keys.at[source, head], key_sems.at[source, head]
        )

    def value_copy(source, head, owner):
        return pltpu.make_async_copy(
            value_refs[owner].at[head], held_values.at[source, head], value_sems.at[source, head]
        )

    for head in range(heads):
        for source, (hops, _, _, odd) in enumerate(jobs):
            if head == 0:
                for place in range(places):
                    pl.when(hops == place)(query_copy(source, place).start)
            for owner in range(2):

                @pl.when(odd == owner)
                def _(head=head, source=source, owner=owner):
                    key_copy(source, head, owner).start()
                    value_copy(source, head, owner).start()

    mark_blocks(marks)
    for source in range(sources):
        count = rows // BLOCK
        held_bias[:, source * count : (source + 1) * count, :] = bias_refs[source][
            :, first_block : first_block + count, :
        ]

    def load_queries(place, head):
        lanes = pl.ds(pl.multiple_of(head * LANES, LANES), LANES)
        block = held_queries[pl.ds(pl.multiple_of(place * tile, tile), tile), lanes]
        bias = [held_bias[head, pl.ds(place * per_tile + j, 1), :] for j in range(per_tile)]
        return widen_queries(block, bias)

    def score_step(queries, source, head, first, target):
        spot = slice(first, first + step)
        keys = jnp.concatenate([held_keys[source, head, spot, :], marks[spot, :]], 1)
        part = lax.dot_general(keys, queries, NT, preferred_element_type=jnp.float32)
        target[spot, :] = part
        return peak_eight(part)

    starts = range(0, tokens, step)

    def one_item(head, place, next_head, next_place, current, upcoming, peaks):
        source, next_source = place // per_source, next_place // per_source
        queries = load_queries(next_place, next_head)
        peak = jnp.maximum(jnp.max(peaks, 0, keepdims=True), LEAST_PEAK)
        peaks = numerator = None
        for first in starts:
            found = score_step(queries, next_source, next_head, first, upcoming)
            peaks = found if peaks is None else jnp.maximum(peaks, found)
            weights = jnp.exp2(current[first : first + step, :] - peak).astype(jnp.bfloat16)
            part = jnp.dot(
                held_values[source, head, :, first : first + step], weights, preferred_element_type=jnp.float32
            )
            numerator = part if numerator is None else numerator + part
        normal, three = finish_rows(numerator, peak)
        columns = pl.ds(pl.multiple_of(place * tile, tile), tile)
        held_out[head, :LANES, columns] = normal
        three = jnp.concatenate([three] * (STAT_ROWS // 4), 0).astype(jnp.bfloat16)
        held_out[head, LANES:, columns] = three
        return peaks

    pairs = tiles // 2

    def one_pair(number, peaks):
        head, place = number // pairs, number % pairs * 2
        peaks = one_item(head, place, head, place + 1, score_a, score_b, peaks)
        is_last = place + 2 == tiles
        next_head = jnp.where(is_last, jnp.minimum(head + 1, heads - 1), head)
        next_place = jnp.where(is_last, 0, place + 2)

        @pl.when(next_head != head)
        def _():
            for source in range(sources):
                key_copy(source, next_head, 0).wait()
                value_copy(source, next_head, 0).wait()

        return one_item(head, place + 1, next_head, next_place, score_b, score_a, peaks)

    query_copy(0, 0).wait()
    key_copy(0, 0, 0).wait()
    queries = load_queries(0, 0)
    peaks = None
    for first in starts:
        found = score_step(queries, 0, 0, first, score_a)
        peaks = found if peaks is None else jnp.maximum(peaks, found)
    query_copy(1, 0).wait()
    key_copy(1, 0, 0).wait()
    for source in range(sources):
        value_copy(source, 0, 0).wait()
    lax.fori_loop(0, heads * pairs, one_pair, peaks)
    copies = []
    last = places - 1

    def send_out(first, count, columns, target, number):
        copies.append(
            pltpu.make_async_copy(
                held_out.at[first, :count, columns],
                target.at[first * LANES : first * LANES + count, :],
                out_sems.at[number, first],
            )
        )
        copies[-1].start()

    both = [slice(source * rows, (source + 1) * rows) for source in range(sources)]
    for source, columns in enumerate(both):
        stats = [held_out[head, LANES : LANES + 4, columns] for head in range(heads)]
        if 4 * heads < STAT_ROWS:
            stats.append(jnp.zeros((STAT_ROWS - 4 * heads, rows), jnp.bfloat16))
        held_out[heads, :STAT_ROWS, columns] = jnp.concatenate(stats, 0)
        for head in range(heads + 1):
            send_out(head, LANES if head < heads else STAT_ROWS, columns, out_refs[source], source)
    joined = slice(sources * rows, (sources + 1) * rows)
    stats = []
    for head in range(heads):
        pieces = []
        for (hops, _, _, _), columns in zip(jobs, both):
            three = held_out[head, LANES : LANES + 3, columns].astype(jnp.float32)
            stat = jnp.sum(three, 0, keepdims=True)
            pieces.append((held_out[head, :LANES, columns], jnp.where(hops == last, stat, NEG_FILL)))
        held_out[head, :LANES, joined], stat = merge_many(pieces)
        stats.append(split_three(stat))
        send_out(head, LANES, joined, joined_ref, sources)
    if 4 * heads < STAT_ROWS:
        stats.append(jnp.zeros((STAT_ROWS - 4 * heads, rows), jnp.float32))
    held_out[heads, :STAT_ROWS, joined] = jnp.concatenate(stats, 0).astype(jnp.bfloat16)
    send_out(heads, STAT_ROWS, joined, joined_ref, sources)
    for copy in copies:
        copy.wait()


def attend_far(info, queries, keys, turned_values, biases, first_block):
    sources = 2
    heads, deep, tokens = turned_values[0].shape
    rows, width = queries[0].shape
    tile = min(256, rows)
    assert rows // tile * sources % 2 == 0 and rows % tile == 0
    anywhere, in_vmem = pl.BlockSpec(memory_space=pl.ANY), pl.BlockSpec(memory_space=pltpu.VMEM)
    return kernel_call(
        functools.partial(
            far_body, places=len(queries), tile=tile, step=min(512, tokens), first_block=first_block
        ),
        "attend_far",
        16,
        in_specs=[pl.BlockSpec(memory_space=pltpu.SMEM)]
        + [anywhere] * (len(queries) + 2 * sources)
        + [in_vmem] * sources,
        out_specs=[anywhere] * (sources + 1),
        out_shape=[jax.ShapeDtypeStruct((heads * LANES + STAT_ROWS, rows), jnp.bfloat16)] * (sources + 1),
        scratch_shapes=[
            pltpu.VMEM((sources * rows, width), jnp.bfloat16),
            pltpu.VMEM((heads, sources * rows // BLOCK, LANES), jnp.float32),
            pltpu.VMEM((sources, heads, tokens, LANES), jnp.bfloat16),
            pltpu.VMEM((sources, heads, deep, tokens), jnp.bfloat16),
            pltpu.VMEM((tokens, LANES), jnp.bfloat16),
            pltpu.VMEM((heads + 1, LANES + STAT_ROWS, (sources + 1) * rows), jnp.bfloat16),
            pltpu.VMEM((tokens, tile), jnp.float32),
            pltpu.VMEM((tokens, tile), jnp.float32),
            pltpu.SemaphoreType.DMA((sources,)),
            pltpu.SemaphoreType.DMA((sources, heads)),
            pltpu.SemaphoreType.DMA((sources, heads)),
            pltpu.SemaphoreType.DMA((sources + 1, heads + 1)),
        ],
    )(info, *queries, *keys, *turned_values, *biases)


def local_body(query_ref, key_ref, value_ref, bias_ref, out_ref, stat_ref, marks, score_a, score_b, *, tile, spots):
    tokens = key_ref.shape[0]
    tiles = tokens // tile
    per_tile = tile // BLOCK
    scores = (score_a, score_b)
    key_place = lax.broadcasted_iota(jnp.int32, (tile, tile), 0)
    query_place = lax.broadcasted_iota(jnp.int32, (tile, tile), 1)
    mark_blocks(marks)
    hidden = (key_place // BLOCK == query_place // BLOCK) & (key_place > query_place)

    def load_queries(place):
        rows = [bias_ref[0, place * per_tile + j : place * per_tile + j + 1, :] for j in range(per_tile)]
        return widen_queries(query_ref[place * tile : (place + 1) * tile, :], rows)

    def score_step(queries, place, number, target):
        spot = slice(number * tile, (number + 1) * tile)
        keys = jnp.concatenate([key_ref[spot, :], marks[spot, :]], 1)
        part = lax.dot_general(keys, queries, NT, preferred_element_type=jnp.float32)
        if number == place:
            part = jnp.where(hidden, NEG_FILL, part)
        target[number * tile : (number + 1) * tile, :] = part
        return peak_eight(part)

    peaks = score_step(load_queries(0), 0, 0, scores[0])
    for place in range(tiles):
        current, upcoming = scores[place % 2], scores[(place + 1) % 2]
        more = place + 1 < tiles
        queries = load_queries(place + 1) if more else None
        peak = jnp.max(peaks, 0, keepdims=True)
        peaks = numerator = None
        for number in range(place + 2):
            if more:
                found = score_step(queries, place + 1, number, upcoming)
                peaks = found if peaks is None else jnp.maximum(peaks, found)
            if number <= place:
                spot = slice(number * tile, (number + 1) * tile)
                weights = jnp.exp2(current[spot, :] - peak).astype(jnp.bfloat16)
                part = jnp.dot(value_ref[0, :, spot], weights, preferred_element_type=jnp.float32)
                numerator = part if numerator is None else numerator + part
        normal, stats = finish_rows(numerator, peak)
        stats = jnp.concatenate([stats] * (STAT_ROWS // 4), 0).astype(jnp.bfloat16)
        for j in range(per_tile):
            columns = pl.ds(spots[place * per_tile + j] * BLOCK, BLOCK)
            out_ref[:, columns] = normal[:, j * BLOCK : (j + 1) * BLOCK]
            stat_ref[0, :, columns] = stats[:, j * BLOCK : (j + 1) * BLOCK]


def attend_local(queries, keys, turned_values, bias, spots):
    tokens = keys.shape[0]
    tile = min(256, tokens)
    blocks = bias.shape[1]
    count = turned_values.shape[0]
    return kernel_call(
        functools.partial(local_body, tile=tile, spots=spots),
        "attend_local",
        18,
        grid=(count,),
        in_specs=[
            pl.BlockSpec((tokens, LANES), lambda h: (0, h)),
            pl.BlockSpec((tokens, LANES), lambda h: (0, h)),
            pl.BlockSpec((1, LANES + STAT_ROWS, tokens), lambda h: (h, 0, 0)),
            pl.BlockSpec((1, blocks, LANES), lambda h: (h, 0, 0)),
        ],
        out_specs=[
            pl.BlockSpec((LANES, tokens), lambda h: (h, 0)),
            pl.BlockSpec((1, STAT_ROWS, tokens), lambda h: (h, 0, 0)),
        ],
        out_shape=[
            jax.ShapeDtypeStruct((count * LANES, tokens), jnp.bfloat16),
            jax.ShapeDtypeStruct((count, STAT_ROWS, tokens), jnp.bfloat16),
        ],
        scratch_shapes=[pltpu.VMEM((tokens, LANES), jnp.bfloat16)]
        + [pltpu.VMEM((tokens, tile), jnp.float32)] * 2,
    )(queries, keys, turned_values, bias)


def packed_stats(ref, heads):
    first = heads * LANES
    return [
        sum(ref[p : p + 1, :].astype(jnp.float32) for p in range(first + 4 * head, first + 4 * head + 3))
        for head in range(heads)
    ]


def merge_many(pieces):
    peak = functools.reduce(jnp.maximum, [stat for _, stat in pieces])
    parts = [jnp.exp2(stat - peak) for _, stat in pieces]
    total = sum(parts)
    mixed = sum(piece.astype(jnp.float32) * (part / total) for (piece, _), part in zip(pieces, parts))
    return mixed.astype(jnp.bfloat16), peak + jnp.log2(total)


def merge_flags(info_ref, hops):
    own = [helper_job(info_ref, number)[0] == hops for number in range(2)]
    return [info_ref[0] >= 2, *own]


def merge_far_body(info_ref, *refs, heads, hops):
    piece_refs, out_ref = refs[:-1], refs[-1]
    flags = merge_flags(info_ref, hops)
    piece_stats = [packed_stats(ref, heads) for ref in piece_refs]
    stats = []
    for head in range(heads):
        rows = slice(head * LANES, (head + 1) * LANES)
        pieces = [
            (ref[rows, :], jnp.where(flag, stat[head], NEG_FILL))
            for ref, stat, flag in zip(piece_refs, piece_stats, flags)
        ]
        out_ref[rows, :], stat = merge_many(pieces)
        stats.append(split_three(stat))
    if 4 * heads < STAT_ROWS:
        stats.append(jnp.zeros((STAT_ROWS - 4 * heads, out_ref.shape[1]), jnp.float32))
    out_ref[heads * LANES :, :] = jnp.concatenate(stats, 0).astype(jnp.bfloat16)


def merge_far(info, pieces, heads, hops):
    in_vmem = pl.BlockSpec(memory_space=pltpu.VMEM)
    return kernel_call(
        functools.partial(merge_far_body, heads=heads, hops=hops),
        "merge_far",
        2.3,
        in_specs=[pl.BlockSpec(memory_space=pltpu.SMEM)] + [in_vmem] * len(pieces),
        out_specs=in_vmem,
        out_shape=jax.ShapeDtypeStruct(pieces[0].shape, jnp.bfloat16),
    )(info, *pieces)


def merge_local_body(info_ref, normal_ref, stat_ref, *refs, heads, stages):
    held_refs, out_ref = refs[:-1], refs[-1]
    others = len(held_refs) // stages
    groups, _, columns = out_ref.shape
    wide = columns // stages
    flags = merge_flags(info_ref, 0)
    slots = []
    for piece in range(groups):
        apart = info_ref[1] ^ piece
        slots.append(jnp.where(info_ref[0] & 1 == 1, bit_reverse(apart, groups.bit_length() - 1), apart))
    for stage in range(stages):
        lanes = slice(stage * groups * wide, (stage + 1) * groups * wide)
        here = held_refs[stage * others : (stage + 1) * others]
        far_stats = [packed_stats(ref, heads) for ref in here]
        for head in range(heads):
            rows = slice(head * LANES, (head + 1) * LANES)
            stat = sum(stat_ref[head, p : p + 1, lanes].astype(jnp.float32) for p in range(3))
            pieces = [(normal_ref[rows, lanes], stat)]
            pieces += [
                (ref[rows, :], jnp.where(flag, far_stat[head], NEG_FILL))
                for ref, far_stat, flag in zip(here, far_stats, flags)
            ]
            held, _ = merge_many(pieces)
            for piece in range(groups):
                out_ref[slots[piece], rows, stage * wide : (stage + 1) * wide] = held[
                    :, piece * wide : (piece + 1) * wide
                ]


def merge_local(info, local, first, stages, chunks, pieces, heads, groups):
    normal, stat = local
    columns = normal.shape[1] // chunks * stages
    assert first % stages == 0
    specs = [
        pl.BlockSpec(memory_space=pltpu.SMEM),
        pl.BlockSpec((normal.shape[0], columns), lambda i: (0, first // stages)),
        pl.BlockSpec((*stat.shape[:2], columns), lambda i: (0, 0, first // stages)),
    ]
    specs += [pl.BlockSpec(piece.shape, lambda i: (0, 0)) for piece in pieces]
    return kernel_call(
        functools.partial(merge_local_body, heads=heads, stages=stages),
        "merge_local",
        4,
        grid=(1,),
        in_specs=specs,
        out_specs=pl.BlockSpec((groups, heads * LANES, columns // groups), lambda i: (0, 0, 0)),
        out_shape=jax.ShapeDtypeStruct((groups, heads * LANES, columns // groups), jnp.bfloat16),
    )(info, normal, stat, *pieces)


def bit_reverse(place, bits):
    return sum((place >> bit & 1) << (bits - 1 - bit) for bit in range(bits))


def project_body(info_ref, weight_ref, *refs, sources, stages, cuts):
    bits = sources.bit_length() - 1
    own_refs, other_refs = refs[: sources - 1], refs[sources - 1 : 2 * sources - 2]
    part_refs = refs[2 * sources - 2 : 2 * sources - 2 + stages * sources]
    out_ref, held, sems = refs[-3:]
    depth, columns = weight_ref.shape
    half = depth // 2
    width = columns // cuts
    parity = info_ref[0] & 1
    copies = []
    for cut in range(cuts):
        lanes = slice(cut * width, (cut + 1) * width)
        pairs = [(weight_ref.at[:, lanes], held.at[cut, :depth, :])]
        for place in range(1, sources):
            own = pl.multiple_of(place * depth + parity * half, half)
            other = pl.multiple_of(bit_reverse(place, bits) * depth + (1 - parity) * half, half)
            pairs.append((own_refs[place - 1].at[:, lanes], held.at[cut, pl.ds(own, half), :]))
            pairs.append((other_refs[place - 1].at[:, lanes], held.at[cut, pl.ds(other, half), :]))
        copies.append(
            [
                pltpu.make_async_copy(origin, target, sems.at[cut, number])
                for number, (origin, target) in enumerate(pairs)
            ]
        )
        for copy in copies[-1]:
            copy.start()
    rows = [
        jnp.concatenate([part_refs[stage * sources + place][...].T for place in range(sources)], 1)
        for stage in range(stages)
    ]
    left = jnp.concatenate(rows, 0)
    for cut in range(cuts):
        for copy in copies[cut]:
            copy.wait()
        out_ref[:, cut * width : (cut + 1) * width] = jnp.dot(
            left, held[cut], preferred_element_type=jnp.float32
        ).astype(jnp.bfloat16)


def project(info, weight_rows, own, other, parts):
    sources, stages, cuts = len(parts[0]), len(parts), 4
    depth, columns = weight_rows.shape
    rows = sum(row[0].shape[1] for row in parts)
    anywhere, in_vmem = pl.BlockSpec(memory_space=pl.ANY), pl.BlockSpec(memory_space=pltpu.VMEM)
    flat = [piece for row in parts for piece in row]
    return kernel_call(
        functools.partial(project_body, sources=sources, stages=stages, cuts=cuts),
        "project",
        15,
        in_specs=[pl.BlockSpec(memory_space=pltpu.SMEM)]
        + [anywhere] * (2 * sources - 1)
        + [in_vmem] * len(flat),
        out_specs=in_vmem,
        out_shape=jax.ShapeDtypeStruct((rows, columns), jnp.bfloat16),
        scratch_shapes=[
            pltpu.VMEM((cuts, sources * depth, columns // cuts), jnp.bfloat16),
            pltpu.SemaphoreType.DMA((cuts, 2 * sources - 1)),
        ],
    )(info, weight_rows, *own, *other, *flat)


def shift(value, steps, first, last):
    return lax.ppermute(value, "ctx", [(source, source + steps) for source in range(first, last)])


def swap_sibling(value):
    return lax.ppermute(value, "ctx", [(i, i ^ 1) for i in range(lax.axis_size("ctx"))])


def swap_head(value, even_bits, odd_bits):
    count = lax.axis_size("head")
    pairs = []
    for place in range(lax.axis_size("ctx")):
        bits = odd_bits if place % 2 else even_bits
        pairs += [(place * count + i, place * count + (i ^ bits)) for i in range(count)]
    return lax.ppermute(value, ("ctx", "head"), pairs)


def gather_weights(weight_rows, parity, earlier):
    count = lax.axis_size("head")
    bits = count.bit_length() - 1
    half = weight_rows.shape[0] // 2
    weight_rows = after(weight_rows, earlier[0])
    held = [lax.dynamic_slice_in_dim(weight_rows, parity * half, half, 0)]
    for number in range(bits):
        sent = [after(piece, earlier[min(number, 1)]) for piece in held]
        held += [swap_head(piece, 1 << number, 1 << (bits - 1 - number)) for piece in sent]
    return held[1:], [swap_sibling(after(piece, earlier[2])) for piece in held[1:]]


def after(value, *earlier):
    return lax.optimization_barrier((value, *earlier))[0]


def chunk_of(array, axis, number, groups, chunks):
    shape = array.shape
    count = shape[axis] // (groups * chunks)
    split = array.reshape(shape[:axis] + (groups, chunks, count) + shape[axis + 1 :])
    piece = lax.index_in_dim(split, number, axis + 1, False)
    return piece.reshape(shape[:axis] + (groups * count,) + shape[axis + 1 :])


def per_device(query_states, key_states, value_states, block_pattern, helper_distances, out_weight):
    count = lax.axis_size("ctx")
    groups = lax.axis_size("head")
    me = lax.axis_index("ctx")
    group = lax.axis_index("head")
    tokens, heads, head_dim = query_states.shape
    blocks = tokens // BLOCK
    chunks = min(4, blocks // groups)
    per_piece = blocks // groups // chunks
    width = heads * head_dim
    parity = me & 1
    bits = groups.bit_length() - 1
    turns = [(place, bit_reverse(place, bits)) for place in range(groups)]
    weight_rows = out_weight.reshape(width, out_weight.shape[2])
    spots = []
    for block in range(blocks):
        part, rest = divmod(block, chunks * per_piece)
        spots.append((rest // per_piece * groups + part) * per_piece + rest % per_piece)

    def flat(array):
        return array.reshape(array.shape[0], width)

    def query_chunk(number):
        return flat(lax.optimization_barrier(chunk_of(query_states, 0, number, groups, chunks)))

    def exchange(pieces):
        return [pieces[0]] + [swap_head(pieces[place], *turns[place]) for place in range(1, groups)]

    places = count // 4
    info = jnp.concatenate([jnp.stack([me, group]), helper_distances])
    hops = [[query_chunk(number)] for number in range(chunks)]

    def move_down(number, *earlier):
        done = len(hops[number])
        moving = after(hops[number][-1], *earlier)
        hops[number].append(shift(moving, -2, 2, count - 2 * (done - 1)))

    for number in range(min(3, chunks)):
        move_down(number)
    keys = flat(key_states)
    turned_values, local_bias, *biases = prepare(info, flat(value_states), block_pattern, spots)
    both_keys = [keys, swap_sibling(keys)]
    both_values = [turned_values, swap_sibling(turned_values)]
    local = attend_local(flat(query_states), keys, turned_values, local_bias, spots)
    for number in range(3, chunks):
        move_down(number, hops[number - 3][1])
    for _ in range(1, places):
        for number in range(chunks):
            move_down(number)

    def attend(number, *earlier):
        arrays = [*hops[number][:-1], after(hops[number][-1], *earlier)]
        return attend_far(info, arrays, both_keys, both_values, biases, number * groups * per_piece)

    def move_up(piece, hops_left):
        return shift(piece, 2, 0, count - 2 * hops_left)

    def finish(first, stages, *earlier):
        pieces = [piece for number in range(first, first + stages) for piece in (moved[number], *own[number])]
        pieces[0] = after(pieces[0], *earlier)
        merged = merge_local(info, local, first, stages, chunks, pieces, heads, groups)
        return merged, exchange(merged)

    own, moved, parts = {}, {}, []
    last = local[0]
    weights = None
    for slot in range(chunks + places - 1):
        if slot < chunks:
            *own[slot], last = attend(slot, last)
            moved[slot] = move_up(last, places)
            if slot == min(1, chunks - 1):
                weights = gather_weights(weight_rows, parity, [local[0], own[0][0], last])
        for behind in range(1, places):
            number = slot - behind
            if 0 <= number < chunks:
                pieces = [after(moved[number], last), *own[number]]
                last = merge_far(info, pieces, heads, places - behind)
                moved[number] = move_up(last, places - behind)
    if chunks > 1:
        last, exchanged = finish(0, chunks - 1, last)
        parts.append(exchanged)
    last, exchanged = finish(chunks - 1, 1, last)
    parts.append(exchanged)
    return project(info, weight_rows, *weights, parts)


def solution(mesh):
    placed = (
        P("ctx", "head", None),
        P("ctx", "head", None),
        P("ctx", "head", None),
        P("head", None, None),
        P(),
        P("head", None, None),
    )
    return jax.shard_map(
        per_device, mesh=mesh, in_specs=placed, out_specs=P(("ctx", "head"), None), check_vma=False
    )
```

```python
import functools

import jax
import jax.numpy as jnp
from jax import lax
from jax.experimental import pallas as pl
from jax.experimental.pallas import tpu as pltpu
from jax.sharding import PartitionSpec as P

BLOCK = 128
LANES = 128
STAT_ROWS = 16
NEG_FILL = -1e30
LEAST_PEAK = -5e29
LOG2E = 1.4426950408889634
NT = (((1,), (1,)), ((), ()))
VMEM_BYTES = 60 * 2**20


def kernel_call(body, name, micros, **options):
    return pl.pallas_call(
        body,
        name=name,
        cost_estimate=pl.CostEstimate(flops=int(micros * 1.15e9), bytes_accessed=1, transcendentals=0),
        compiler_params=pltpu.CompilerParams(vmem_limit_bytes=VMEM_BYTES),
        **options,
    )


def helper_job(info_ref, number):
    me, distance = info_ref[0], info_ref[2 + number]
    odd = distance & 1
    hops = (distance + odd * (1 - 2 * (me & 1))) >> 1
    query_shard = me + 2 * hops
    return hops, query_shard, query_shard - distance, odd


def bias_rows(pattern_ref, query_shard, key_shard, blocks, is_local):
    count = pattern_ref.shape[1] // blocks
    query_shard = jnp.clip(query_shard, 0, count - 1)
    key_shard = jnp.clip(key_shard, 0, count - 1)
    rows = pattern_ref[0, pl.ds(pl.multiple_of(query_shard * blocks, blocks), blocks), :]
    width = rows.shape[1]
    rows = pltpu.roll(rows, width - key_shard * blocks, 1)
    if width >= LANES:
        rows = rows[:, :LANES]
    else:
        rows = jnp.concatenate([rows, jnp.zeros((blocks, LANES - width), rows.dtype)], 1)
    query_block = lax.broadcasted_iota(jnp.int32, rows.shape, 0)
    key_block = lax.broadcasted_iota(jnp.int32, rows.shape, 1)
    seen = rows > 0
    if is_local:
        seen = seen & (key_block < query_block) | (key_block == query_block)
    return jnp.where(seen | (key_block >= blocks), 0.0, NEG_FILL)


def mark_blocks(ref):
    block_of = lax.broadcasted_iota(jnp.int32, ref.shape, 0) // BLOCK
    lane = lax.broadcasted_iota(jnp.int32, ref.shape, 1)
    ref[...] = jnp.where(block_of == lane, 1.0, 0.0).astype(jnp.bfloat16)


def prepare_body(info_ref, value_ref, pattern_ref, turned_value_ref, local_ref, *bias_refs, spots):
    tokens = value_ref.shape[0]
    turned_value_ref[0, :LANES, :] = value_ref[...].T
    turned_value_ref[0, LANES:, :] = jnp.ones((STAT_ROWS, tokens), jnp.bfloat16)
    local_ref[0] = bias_rows(pattern_ref, info_ref[0], info_ref[0], len(spots), True)
    for number, out_ref in enumerate(bias_refs):
        _, query_shard, key_shard, _ = helper_job(info_ref, number)
        rows = bias_rows(pattern_ref, query_shard, key_shard, len(spots), False)
        for block, spot in enumerate(spots):
            out_ref[0, spot : spot + 1, :] = rows[block : block + 1, :]


def prepare(info, values, block_pattern, spots):
    tokens, width = values.shape
    heads = width // LANES
    out_shapes = [(LANES + STAT_ROWS, tokens)] + [(len(spots), LANES)] * 3
    out_types = [jnp.bfloat16] + [jnp.float32] * 3
    return kernel_call(
        functools.partial(prepare_body, spots=spots),
        "prepare",
        4,
        grid=(heads,),
        in_specs=[
            pl.BlockSpec(memory_space=pltpu.SMEM),
            pl.BlockSpec((tokens, LANES), lambda h: (0, h)),
            pl.BlockSpec((1, *block_pattern.shape[1:]), lambda h: (h, 0, 0)),
        ],
        out_specs=[pl.BlockSpec((1, *shape), lambda h: (h, 0, 0)) for shape in out_shapes],
        out_shape=[
            jax.ShapeDtypeStruct((heads, *shape), kind) for shape, kind in zip(out_shapes, out_types)
        ],
    )(info, values, block_pattern)


def widen_queries(queries, bias_rows):
    scaled = (queries.astype(jnp.float32) * (LANES**-0.5 * LOG2E)).astype(jnp.bfloat16)
    rows = queries.shape[0] // len(bias_rows)
    bias = [jnp.broadcast_to(row, (rows, LANES)).astype(jnp.bfloat16) for row in bias_rows]
    return jnp.concatenate([scaled, jnp.concatenate(bias, 0)], 1)


def split_three(value):
    high = value.astype(jnp.bfloat16).astype(jnp.float32)
    rest = value - high
    middle = rest.astype(jnp.bfloat16).astype(jnp.float32)
    low = rest - middle
    return jnp.concatenate([high, middle, low, jnp.zeros_like(low)], 0)


def peak_eight(scores):
    return jnp.max(scores.reshape(scores.shape[0] // 8, 8, scores.shape[1]), 0)


def finish_rows(numerator, peak):
    total = jnp.maximum(numerator[LANES : LANES + 1], 1e-30)
    normal = (numerator[:LANES] * (1.0 / total)).astype(jnp.bfloat16)
    return normal, split_three(peak + jnp.log2(total))


def far_body(info_ref, *refs, places, tile, step, first_block):
    sources = 2
    query_refs, refs = refs[:places], refs[places:]
    key_refs, value_refs, bias_refs, out_refs, joined_ref, refs = (
        refs[:2],
        refs[2:4],
        refs[4:6],
        refs[6:8],
        refs[8],
        refs[9:],
    )
    (
        held_queries,
        held_bias,
        held_keys,
        held_values,
        marks,
        held_out,
        score_a,
        score_b,
        query_sems,
        key_sems,
        value_sems,
        out_sems,
    ) = refs
    heads, _, tokens = value_refs[0].shape
    jobs = [helper_job(info_ref, number) for number in range(sources)]
    rows = query_refs[0].shape[0]
    tiles = sources * rows // tile
    per_tile = tile // BLOCK
    per_source = rows // tile
    scores = (score_a, score_b)

    def query_copy(source, place):
        target = held_queries.at[source * rows : (source + 1) * rows, :]
        return pltpu.make_async_copy(query_refs[place], target, query_sems.at[source])

    def key_copy(source, head, owner):
        lanes = pl.ds(pl.multiple_of(head * LANES, LANES), LANES)
        return pltpu.make_async_copy(
            key_refs[owner].at[:, lanes], held_keys.at[source, head], key_sems.at[source, head]
        )

    def value_copy(source, head, owner):
        return pltpu.make_async_copy(
            value_refs[owner].at[head], held_values.at[source, head], value_sems.at[source, head]
        )

    def start_head(head):
        for source, (_, _, _, odd) in enumerate(jobs):
            for owner in range(2):

                @pl.when(odd == owner)
                def _(source=source, owner=owner):
                    key_copy(source, head, owner).start()
                    value_copy(source, head, owner).start()

    for source, (hops, _, _, _) in enumerate(jobs):
        for place in range(places):
            pl.when(jnp.minimum(hops, places - 1) == place)(query_copy(source, place).start)
    start_head(0)
    mark_blocks(marks)
    for source in range(sources):
        count = rows // BLOCK
        held_bias[:, source * count : (source + 1) * count, :] = bias_refs[source][
            :, first_block : first_block + count, :
        ]

    def load_queries(place, head):
        lanes = pl.ds(pl.multiple_of(head * LANES, LANES), LANES)
        block = held_queries[pl.ds(pl.multiple_of(place * tile, tile), tile), lanes]
        bias = [held_bias[head, pl.ds(place * per_tile + j, 1), :] for j in range(per_tile)]
        return widen_queries(block, bias)

    def score_step(queries, source, head, first, target):
        spot = slice(first, first + step)
        keys = jnp.concatenate([held_keys[source, head, spot, :], marks[spot, :]], 1)
        part = lax.dot_general(keys, queries, NT, preferred_element_type=jnp.float32)
        target[spot, :] = part
        return peak_eight(part)

    starts = range(0, tokens, step)

    def one_item(head, place, next_head, next_place, current, upcoming, peaks):
        source, next_source = place // per_source, next_place // per_source
        queries = load_queries(next_place, next_head)
        peak = jnp.maximum(jnp.max(peaks, 0, keepdims=True), LEAST_PEAK)
        peaks = numerator = None
        for first in starts:
            found = score_step(queries, next_source, next_head, first, upcoming)
            peaks = found if peaks is None else jnp.maximum(peaks, found)
            weights = jnp.exp2(current[first : first + step, :] - peak).astype(jnp.bfloat16)
            part = jnp.dot(
                held_values[source, head, :, first : first + step], weights, preferred_element_type=jnp.float32
            )
            numerator = part if numerator is None else numerator + part
        normal, three = finish_rows(numerator, peak)
        columns = pl.ds(pl.multiple_of(place * tile, tile), tile)
        held_out[head, :LANES, columns] = normal
        three = jnp.concatenate([three] * (STAT_ROWS // 4), 0).astype(jnp.bfloat16)
        held_out[head, LANES:, columns] = three
        return peaks

    pairs = tiles // 2

    def one_pair(number, peaks):
        head, place = number // pairs, number % pairs * 2
        peaks = one_item(head, place, head, place + 1, score_a, score_b, peaks)
        is_last = place + 2 == tiles
        next_head = jnp.where(is_last, jnp.minimum(head + 1, heads - 1), head)
        next_place = jnp.where(is_last, 0, place + 2)

        @pl.when(next_head != head)
        def _():
            for source in range(sources):
                key_copy(source, next_head, 0).wait()
                value_copy(source, next_head, 0).wait()

        return one_item(head, place + 1, next_head, next_place, score_b, score_a, peaks)

    query_copy(0, 0).wait()
    key_copy(0, 0, 0).wait()
    queries = load_queries(0, 0)
    peaks = None
    for first in starts:
        found = score_step(queries, 0, 0, first, score_a)
        peaks = found if peaks is None else jnp.maximum(peaks, found)
    query_copy(1, 0).wait()
    key_copy(1, 0, 0).wait()
    for source in range(sources):
        value_copy(source, 0, 0).wait()
    for head in range(1, heads):
        start_head(head)
    lax.fori_loop(0, heads * pairs, one_pair, peaks)
    copies = []
    last = places - 1

    def send_out(first, count, columns, target, number):
        copies.append(
            pltpu.make_async_copy(
                held_out.at[first, :count, columns],
                target.at[first * LANES : first * LANES + count, :],
                out_sems.at[number, first],
            )
        )
        copies[-1].start()

    both = [slice(source * rows, (source + 1) * rows) for source in range(sources)]
    for source, columns in enumerate(both):
        stats = [held_out[head, LANES : LANES + 4, columns] for head in range(heads)]
        if 4 * heads < STAT_ROWS:
            stats.append(jnp.zeros((STAT_ROWS - 4 * heads, rows), jnp.bfloat16))
        held_out[heads, :STAT_ROWS, columns] = jnp.concatenate(stats, 0)
        for head in range(heads + 1):
            send_out(head, LANES if head < heads else STAT_ROWS, columns, out_refs[source], source)
    joined = slice(sources * rows, (sources + 1) * rows)
    stats = []
    for head in range(heads):
        pieces = []
        for (hops, _, _, _), columns in zip(jobs, both):
            three = held_out[head, LANES : LANES + 3, columns].astype(jnp.float32)
            stat = jnp.sum(three, 0, keepdims=True)
            pieces.append((held_out[head, :LANES, columns], jnp.where(hops == last, stat, NEG_FILL)))
        held_out[head, :LANES, joined], stat = merge_many(pieces)
        stats.append(split_three(stat))
        send_out(head, LANES, joined, joined_ref, sources)
    if 4 * heads < STAT_ROWS:
        stats.append(jnp.zeros((STAT_ROWS - 4 * heads, rows), jnp.float32))
    held_out[heads, :STAT_ROWS, joined] = jnp.concatenate(stats, 0).astype(jnp.bfloat16)
    send_out(heads, STAT_ROWS, joined, joined_ref, sources)
    for copy in copies:
        copy.wait()


def attend_far(info, queries, keys, turned_values, biases, first_block):
    sources = 2
    heads, deep, tokens = turned_values[0].shape
    rows, width = queries[0].shape
    tile = min(256, rows)
    assert rows // tile * sources % 2 == 0 and rows % tile == 0
    anywhere, in_vmem = pl.BlockSpec(memory_space=pl.ANY), pl.BlockSpec(memory_space=pltpu.VMEM)
    return kernel_call(
        functools.partial(
            far_body, places=len(queries), tile=tile, step=min(512, tokens), first_block=first_block
        ),
        "attend_far",
        16,
        in_specs=[pl.BlockSpec(memory_space=pltpu.SMEM)]
        + [anywhere] * (len(queries) + 2 * sources)
        + [in_vmem] * sources,
        out_specs=[anywhere] * (sources + 1),
        out_shape=[jax.ShapeDtypeStruct((heads * LANES + STAT_ROWS, rows), jnp.bfloat16)] * (sources + 1),
        scratch_shapes=[
            pltpu.VMEM((sources * rows, width), jnp.bfloat16),
            pltpu.VMEM((heads, sources * rows // BLOCK, LANES), jnp.float32),
            pltpu.VMEM((sources, heads, tokens, LANES), jnp.bfloat16),
            pltpu.VMEM((sources, heads, deep, tokens), jnp.bfloat16),
            pltpu.VMEM((tokens, LANES), jnp.bfloat16),
            pltpu.VMEM((heads + 1, LANES + STAT_ROWS, (sources + 1) * rows), jnp.bfloat16),
            pltpu.VMEM((tokens, tile), jnp.float32),
            pltpu.VMEM((tokens, tile), jnp.float32),
            pltpu.SemaphoreType.DMA((sources,)),
            pltpu.SemaphoreType.DMA((sources, heads)),
            pltpu.SemaphoreType.DMA((sources, heads)),
            pltpu.SemaphoreType.DMA((sources + 1, heads + 1)),
        ],
    )(info, *queries, *keys, *turned_values, *biases)


def local_body(query_ref, key_ref, value_ref, bias_ref, out_ref, stat_ref, marks, score_a, score_b, *, tile, spots):
    tokens = key_ref.shape[0]
    tiles = tokens // tile
    per_tile = tile // BLOCK
    scores = (score_a, score_b)
    key_place = lax.broadcasted_iota(jnp.int32, (tile, tile), 0)
    query_place = lax.broadcasted_iota(jnp.int32, (tile, tile), 1)
    mark_blocks(marks)
    hidden = (key_place // BLOCK == query_place // BLOCK) & (key_place > query_place)

    def load_queries(place):
        rows = [bias_ref[0, place * per_tile + j : place * per_tile + j + 1, :] for j in range(per_tile)]
        return widen_queries(query_ref[place * tile : (place + 1) * tile, :], rows)

    def score_step(queries, place, number, target):
        spot = slice(number * tile, (number + 1) * tile)
        keys = jnp.concatenate([key_ref[spot, :], marks[spot, :]], 1)
        part = lax.dot_general(keys, queries, NT, preferred_element_type=jnp.float32)
        if number == place:
            part = jnp.where(hidden, NEG_FILL, part)
        target[number * tile : (number + 1) * tile, :] = part
        return peak_eight(part)

    peaks = score_step(load_queries(0), 0, 0, scores[0])
    for place in range(tiles):
        current, upcoming = scores[place % 2], scores[(place + 1) % 2]
        more = place + 1 < tiles
        queries = load_queries(place + 1) if more else None
        peak = jnp.max(peaks, 0, keepdims=True)
        peaks = numerator = None
        for number in range(place + 2):
            if more:
                found = score_step(queries, place + 1, number, upcoming)
                peaks = found if peaks is None else jnp.maximum(peaks, found)
            if number <= place:
                spot = slice(number * tile, (number + 1) * tile)
                weights = jnp.exp2(current[spot, :] - peak).astype(jnp.bfloat16)
                part = jnp.dot(value_ref[0, :, spot], weights, preferred_element_type=jnp.float32)
                numerator = part if numerator is None else numerator + part
        normal, stats = finish_rows(numerator, peak)
        stats = jnp.concatenate([stats] * (STAT_ROWS // 4), 0).astype(jnp.bfloat16)
        for j in range(per_tile):
            columns = pl.ds(spots[place * per_tile + j] * BLOCK, BLOCK)
            out_ref[:, columns] = normal[:, j * BLOCK : (j + 1) * BLOCK]
            stat_ref[0, :, columns] = stats[:, j * BLOCK : (j + 1) * BLOCK]


def attend_local(queries, keys, turned_values, bias, spots, head, count):
    tokens = keys.shape[0]
    tile = min(256, tokens)
    blocks = bias.shape[1]
    return kernel_call(
        functools.partial(local_body, tile=tile, spots=spots),
        "attend_local",
        10,
        grid=(count,),
        in_specs=[
            pl.BlockSpec((tokens, LANES), lambda h: (0, head + h)),
            pl.BlockSpec((tokens, LANES), lambda h: (0, head + h)),
            pl.BlockSpec((1, LANES + STAT_ROWS, tokens), lambda h: (head + h, 0, 0)),
            pl.BlockSpec((1, blocks, LANES), lambda h: (head + h, 0, 0)),
        ],
        out_specs=[
            pl.BlockSpec((LANES, tokens), lambda h: (h, 0)),
            pl.BlockSpec((1, STAT_ROWS, tokens), lambda h: (h, 0, 0)),
        ],
        out_shape=[
            jax.ShapeDtypeStruct((count * LANES, tokens), jnp.bfloat16),
            jax.ShapeDtypeStruct((count, STAT_ROWS, tokens), jnp.bfloat16),
        ],
        scratch_shapes=[pltpu.VMEM((tokens, LANES), jnp.bfloat16)]
        + [pltpu.VMEM((tokens, tile), jnp.float32)] * 2,
    )(queries, keys, turned_values, bias)


def packed_stats(ref, heads):
    first = heads * LANES
    return [
        sum(ref[p : p + 1, :].astype(jnp.float32) for p in range(first + 4 * head, first + 4 * head + 3))
        for head in range(heads)
    ]


def merge_many(pieces):
    peak = functools.reduce(jnp.maximum, [stat for _, stat in pieces])
    parts = [jnp.exp2(stat - peak) for _, stat in pieces]
    total = sum(parts)
    mixed = sum(piece.astype(jnp.float32) * (part / total) for (piece, _), part in zip(pieces, parts))
    return mixed.astype(jnp.bfloat16), peak + jnp.log2(total)


def merge_flags(info_ref, hops):
    own = [helper_job(info_ref, number)[0] == hops for number in range(2)]
    return [info_ref[0] >= 2, *own]


def merge_far_body(info_ref, *refs, heads, hops):
    piece_refs, out_ref = refs[:-1], refs[-1]
    flags = merge_flags(info_ref, hops)
    piece_stats = [packed_stats(ref, heads) for ref in piece_refs]
    stats = []
    for head in range(heads):
        rows = slice(head * LANES, (head + 1) * LANES)
        pieces = [
            (ref[rows, :], jnp.where(flag, stat[head], NEG_FILL))
            for ref, stat, flag in zip(piece_refs, piece_stats, flags)
        ]
        out_ref[rows, :], stat = merge_many(pieces)
        stats.append(split_three(stat))
    if 4 * heads < STAT_ROWS:
        stats.append(jnp.zeros((STAT_ROWS - 4 * heads, out_ref.shape[1]), jnp.float32))
    out_ref[heads * LANES :, :] = jnp.concatenate(stats, 0).astype(jnp.bfloat16)


def merge_far(info, pieces, heads, hops):
    in_vmem = pl.BlockSpec(memory_space=pltpu.VMEM)
    return kernel_call(
        functools.partial(merge_far_body, heads=heads, hops=hops),
        "merge_far",
        40,
        in_specs=[pl.BlockSpec(memory_space=pltpu.SMEM)] + [in_vmem] * len(pieces),
        out_specs=in_vmem,
        out_shape=jax.ShapeDtypeStruct(pieces[0].shape, jnp.bfloat16),
    )(info, *pieces)


def merge_local_body(info_ref, *refs, heads, runs, stages, groups):
    local_refs, held_refs = refs[: 2 * runs], refs[2 * runs : -1 - groups]
    out_refs, turned_ref = refs[-1 - groups : -1], refs[-1]
    per_run = heads // runs
    others = len(held_refs) // stages
    wide = out_refs[0].shape[0] // stages
    flags = merge_flags(info_ref, 0)
    for stage in range(stages):
        lanes = slice(stage * groups * wide, (stage + 1) * groups * wide)
        here = held_refs[stage * others : (stage + 1) * others]
        far_stats = [packed_stats(ref, heads) for ref in here]
        for head in range(heads):
            rows = slice(head * LANES, (head + 1) * LANES)
            normal_ref, stat_ref = local_refs[2 * (head // per_run) : 2 * (head // per_run) + 2]
            spot = head % per_run
            stat = sum(stat_ref[spot, p : p + 1, lanes].astype(jnp.float32) for p in range(3))
            pieces = [(normal_ref[spot * LANES : (spot + 1) * LANES, lanes], stat)]
            pieces += [
                (ref[rows, :], jnp.where(flag, far_stat[head], NEG_FILL))
                for ref, far_stat, flag in zip(here, far_stats, flags)
            ]
            turned_ref[:, rows] = merge_many(pieces)[0].T
        for place, out_ref in enumerate(out_refs):
            apart = jnp.where(info_ref[0] & 1 == 1, bit_reverse(place, groups.bit_length() - 1), place)
            first = pl.multiple_of((info_ref[1] ^ apart) * wide, wide)
            out_ref[stage * wide : (stage + 1) * wide, :] = turned_ref[pl.ds(first, wide), :]


def merge_local(info, local, first, stages, chunks, pieces, heads, groups):
    columns = local[0][0].shape[1] // chunks * stages
    assert first % stages == 0
    specs = [pl.BlockSpec(memory_space=pltpu.SMEM)]
    for normal, stat in local:
        specs += [
            pl.BlockSpec((normal.shape[0], columns), lambda i: (0, first // stages)),
            pl.BlockSpec((*stat.shape[:2], columns), lambda i: (0, 0, first // stages)),
        ]
    specs += [pl.BlockSpec(piece.shape, lambda i: (0, 0)) for piece in pieces]
    return kernel_call(
        functools.partial(
            merge_local_body, heads=heads, runs=len(local), stages=stages, groups=groups
        ),
        "merge_local",
        40,
        grid=(1,),
        in_specs=specs,
        out_specs=[pl.BlockSpec((columns // groups, heads * LANES), lambda i: (0, 0))] * groups,
        out_shape=[jax.ShapeDtypeStruct((columns // groups, heads * LANES), jnp.bfloat16)] * groups,
        scratch_shapes=[pltpu.VMEM((columns // stages, heads * LANES), jnp.bfloat16)],
    )(info, *[array for both in local for array in both], *pieces)


def bit_reverse(place, bits):
    return sum((place >> bit & 1) << (bits - 1 - bit) for bit in range(bits))


def project_body(info_ref, weight_ref, *refs, sources, stages, cuts):
    bits = sources.bit_length() - 1
    own_refs, other_refs = refs[: sources - 1], refs[sources - 1 : 2 * sources - 2]
    part_refs = refs[2 * sources - 2 : 2 * sources - 2 + stages * sources]
    out_ref, held, outs, sems, out_sems = refs[-5:]
    depth, columns = weight_ref.shape
    half = depth // 2
    width = columns // cuts
    parity = info_ref[0] & 1
    copies = []
    for cut in range(cuts):
        lanes = slice(cut * width, (cut + 1) * width)
        pairs = [(weight_ref.at[:, lanes], held.at[cut, :depth, :])]
        for place in range(1, sources):
            own = pl.multiple_of(place * depth + parity * half, half)
            other = pl.multiple_of(bit_reverse(place, bits) * depth + (1 - parity) * half, half)
            pairs.append((own_refs[place - 1].at[:, lanes], held.at[cut, pl.ds(own, half), :]))
            pairs.append((other_refs[place - 1].at[:, lanes], held.at[cut, pl.ds(other, half), :]))
        copies.append(
            [
                pltpu.make_async_copy(origin, target, sems.at[cut, number])
                for number, (origin, target) in enumerate(pairs)
            ]
        )
        for copy in copies[-1]:
            copy.start()
    rows = [
        jnp.concatenate([part_refs[stage * sources + place][...] for place in range(sources)], 1)
        for stage in range(stages)
    ]
    left = jnp.concatenate(rows, 0)
    out_copies = []
    for cut in range(cuts):
        for copy in copies[cut]:
            copy.wait()
        outs[cut] = jnp.dot(left, held[cut], preferred_element_type=jnp.float32).astype(jnp.bfloat16)
        out_copies.append(
            pltpu.make_async_copy(
                outs.at[cut], out_ref.at[:, cut * width : (cut + 1) * width], out_sems.at[cut]
            )
        )
        out_copies[-1].start()
    for copy in out_copies:
        copy.wait()


def project(info, weight_rows, own, other, parts):
    sources, stages, cuts = len(parts[0]), len(parts), 4
    depth, columns = weight_rows.shape
    rows = sum(row[0].shape[0] for row in parts)
    anywhere, in_vmem = pl.BlockSpec(memory_space=pl.ANY), pl.BlockSpec(memory_space=pltpu.VMEM)
    flat = [piece for row in parts for piece in row]
    return kernel_call(
        functools.partial(project_body, sources=sources, stages=stages, cuts=cuts),
        "project",
        15,
        in_specs=[pl.BlockSpec(memory_space=pltpu.SMEM)]
        + [anywhere] * (2 * sources - 1)
        + [in_vmem] * len(flat),
        out_specs=anywhere,
        out_shape=jax.ShapeDtypeStruct((rows, columns), jnp.bfloat16),
        scratch_shapes=[
            pltpu.VMEM((cuts, sources * depth, columns // cuts), jnp.bfloat16),
            pltpu.VMEM((cuts, rows, columns // cuts), jnp.bfloat16),
            pltpu.SemaphoreType.DMA((cuts, 2 * sources - 1)),
            pltpu.SemaphoreType.DMA((cuts,)),
        ],
    )(info, weight_rows, *own, *other, *flat)


def shift(value, steps, first, last):
    return lax.ppermute(value, "ctx", [(source, source + steps) for source in range(first, last)])


def swap_sibling(value):
    return lax.ppermute(value, "ctx", [(i, i ^ 1) for i in range(lax.axis_size("ctx"))])


def swap_head(value, even_bits, odd_bits):
    count = lax.axis_size("head")
    pairs = []
    for place in range(lax.axis_size("ctx")):
        bits = odd_bits if place % 2 else even_bits
        pairs += [(place * count + i, place * count + (i ^ bits)) for i in range(count)]
    return lax.ppermute(value, ("ctx", "head"), pairs)


def start_weights(weight_rows, parity, *earlier):
    half = weight_rows.shape[0] // 2
    return [lax.dynamic_slice_in_dim(after(weight_rows, *earlier), parity * half, half, 0)]


def double_weights(held, *earlier):
    bits = lax.axis_size("head").bit_length() - 1
    number = len(held).bit_length() - 1
    sent = [after(piece, *earlier) for piece in held]
    return held + [swap_head(piece, 1 << number, 1 << (bits - 1 - number)) for piece in sent]


def after(value, *earlier):
    return lax.optimization_barrier((value, *earlier))[0]


def chunk_of(array, axis, number, groups, chunks):
    shape = array.shape
    count = shape[axis] // (groups * chunks)
    split = array.reshape(shape[:axis] + (groups, chunks, count) + shape[axis + 1 :])
    piece = lax.index_in_dim(split, number, axis + 1, False)
    return piece.reshape(shape[:axis] + (groups * count,) + shape[axis + 1 :])


def per_device(query_states, key_states, value_states, block_pattern, helper_distances, out_weight):
    count = lax.axis_size("ctx")
    groups = lax.axis_size("head")
    me = lax.axis_index("ctx")
    group = lax.axis_index("head")
    tokens, heads, head_dim = query_states.shape
    blocks = tokens // BLOCK
    chunks = min(4, blocks // groups)
    per_piece = blocks // groups // chunks
    width = heads * head_dim
    parity = me & 1
    bits = groups.bit_length() - 1
    turns = [(place, bit_reverse(place, bits)) for place in range(groups)]
    weight_rows = out_weight.reshape(width, out_weight.shape[2])
    spots = []
    for block in range(blocks):
        part, rest = divmod(block, chunks * per_piece)
        spots.append((rest // per_piece * groups + part) * per_piece + rest % per_piece)

    def flat(array):
        return array.reshape(array.shape[0], width)

    def query_chunk(number):
        return flat(lax.optimization_barrier(chunk_of(query_states, 0, number, groups, chunks)))

    def exchange(pieces):
        return [pieces[0]] + [swap_head(pieces[place], *turns[place]) for place in range(1, groups)]

    places = count // 4
    info = jnp.concatenate([jnp.stack([me, group]), helper_distances])
    hops = [[query_chunk(number)] for number in range(chunks)]

    def move_down(number, *earlier):
        done = len(hops[number])
        moving = after(hops[number][-1], *earlier)
        hops[number].append(shift(moving, -2, 2, count - 2 * (done - 1)))

    for number in range(min(2, chunks)):
        move_down(number)
    keys = flat(key_states)
    turned_values, local_bias, *biases = prepare(info, flat(value_states), block_pattern, spots)
    both_keys = [keys, swap_sibling(keys)]
    both_values = [turned_values, swap_sibling(turned_values)]
    queries = flat(query_states)
    half = heads // 2
    for _ in range(1, places):
        move_down(0)
    local = [attend_local(queries, keys, turned_values, local_bias, spots, 0, half)]
    queries = after(queries, local[0][0], hops[0][-1])
    local.append(attend_local(queries, keys, turned_values, local_bias, spots, half, half))
    for number in range(2, chunks):
        move_down(number, local[number % 2][0])

    def attend(number, *earlier):
        arrays = [*hops[number][:-1], after(hops[number][-1], *earlier)]
        return attend_far(info, arrays, both_keys, both_values, biases, number * groups * per_piece)

    def move_up(piece, hops_left):
        return shift(piece, 2, 0, count - 2 * hops_left)

    def finish(first, stages, *earlier):
        pieces = [piece for number in range(first, first + stages) for piece in (moved[number], *own[number])]
        pieces[0] = after(pieces[0], *earlier)
        merged = merge_local(info, local, first, stages, chunks, pieces, heads, groups)
        return merged[0], exchange(merged)

    own, moved, parts = {}, {}, []
    last = local[1][0]
    held = double_weights(start_weights(weight_rows, parity, hops[0][1]))
    waits = {0: held[1:]}
    while len(held) < groups:
        first = len(held)
        held = double_weights(held)
        waits[1], waits[3] = waits.get(1, []) + held[first : first + 1], held[first + 1 :]
    other = [swap_sibling(piece) for piece in held[1:]]
    for slot in range(chunks + places - 1):
        for number in [1, 2] if slot == 0 else [slot + 2]:
            for _ in range(1, places if number < chunks else 1):
                move_down(number, last)
        if slot < chunks:
            arrived = waits.get(slot, [])
            *own[slot], last = attend(slot, last, *arrived)
            moved[slot] = move_up(last, places)
        for behind in range(1, places):
            number = slot - behind
            if 0 <= number < chunks:
                waited = [moved[number - 1]] if 0 < number < chunks - 1 else []
                pieces = [after(moved[number], last, *waited), *own[number]]
                last = merge_far(info, pieces, heads, places - behind)
                moved[number] = move_up(last, places - behind)
                if number == chunks - 2 and chunks == 4 and places == 2:
                    last, exchanged = finish(0, 2, last)
                    parts.append(exchanged)
    done = sum(row[0].shape[0] for row in parts) * chunks * groups // tokens
    for number in range(done, chunks):
        waited = [*(parts[-1] if parts else []), *(other if number == done else [])]
        last, exchanged = finish(number, 1, last, *waited)
        parts.append(exchanged)
    return project(info, weight_rows, held[1:], other, parts)


def solution(mesh):
    placed = (
        P("ctx", "head", None),
        P("ctx", "head", None),
        P("ctx", "head", None),
        P("head", None, None),
        P(),
        P("head", None, None),
    )
    return jax.shard_map(
        per_device, mesh=mesh, in_specs=placed, out_specs=P(("ctx", "head"), None), check_vma=False
    )
```

```python
import functools

import jax
import jax.numpy as jnp
from jax import lax
from jax.experimental import pallas as pl
from jax.experimental.pallas import tpu as pltpu
from jax.sharding import PartitionSpec as P

BLOCK = 128
LANES = 128
STAT_ROWS = 16
NEG_FILL = -1e30
LEAST_PEAK = -5e29
LOG2E = 1.4426950408889634
NT = (((1,), (1,)), ((), ()))
VMEM_BYTES = 60 * 2**20


def kernel_call(body, name, micros, **options):
    return pl.pallas_call(
        body,
        name=name,
        cost_estimate=pl.CostEstimate(flops=int(micros * 1.15e9), bytes_accessed=1, transcendentals=0),
        compiler_params=pltpu.CompilerParams(vmem_limit_bytes=VMEM_BYTES),
        **options,
    )


def helper_job(info_ref, number):
    me, distance = info_ref[0], info_ref[2 + number]
    odd = distance & 1
    hops = (distance + odd * (1 - 2 * (me & 1))) >> 1
    query_shard = me + 2 * hops
    return hops, query_shard, query_shard - distance, odd


def bias_rows(pattern_ref, query_shard, key_shard, blocks, is_local):
    count = pattern_ref.shape[1] // blocks
    query_shard = jnp.clip(query_shard, 0, count - 1)
    key_shard = jnp.clip(key_shard, 0, count - 1)
    rows = pattern_ref[0, pl.ds(pl.multiple_of(query_shard * blocks, blocks), blocks), :]
    width = rows.shape[1]
    rows = pltpu.roll(rows, width - key_shard * blocks, 1)
    if width >= LANES:
        rows = rows[:, :LANES]
    else:
        rows = jnp.concatenate([rows, jnp.zeros((blocks, LANES - width), rows.dtype)], 1)
    query_block = lax.broadcasted_iota(jnp.int32, rows.shape, 0)
    key_block = lax.broadcasted_iota(jnp.int32, rows.shape, 1)
    seen = rows > 0
    if is_local:
        seen = seen & (key_block < query_block) | (key_block == query_block)
    return jnp.where(seen | (key_block >= blocks), 0.0, NEG_FILL)


def mark_blocks(ref):
    block_of = lax.broadcasted_iota(jnp.int32, ref.shape, 0) // BLOCK
    lane = lax.broadcasted_iota(jnp.int32, ref.shape, 1)
    ref[...] = jnp.where(block_of == lane, 1.0, 0.0).astype(jnp.bfloat16)


def prepare_body(info_ref, value_ref, pattern_ref, turned_value_ref, local_ref, *bias_refs, spots):
    tokens = value_ref.shape[0]
    turned_value_ref[0, :LANES, :] = value_ref[...].T
    turned_value_ref[0, LANES:, :] = jnp.ones((STAT_ROWS, tokens), jnp.bfloat16)
    local_ref[0] = bias_rows(pattern_ref, info_ref[0], info_ref[0], len(spots), True)
    for number, out_ref in enumerate(bias_refs):
        _, query_shard, key_shard, _ = helper_job(info_ref, number)
        rows = bias_rows(pattern_ref, query_shard, key_shard, len(spots), False)
        for block, spot in enumerate(spots):
            out_ref[0, spot : spot + 1, :] = rows[block : block + 1, :]


def prepare(info, values, block_pattern, spots):
    tokens, width = values.shape
    heads = width // LANES
    out_shapes = [(LANES + STAT_ROWS, tokens)] + [(len(spots), LANES)] * 3
    out_types = [jnp.bfloat16] + [jnp.float32] * 3
    return kernel_call(
        functools.partial(prepare_body, spots=spots),
        "prepare",
        4,
        grid=(heads,),
        in_specs=[
            pl.BlockSpec(memory_space=pltpu.SMEM),
            pl.BlockSpec((tokens, LANES), lambda h: (0, h)),
            pl.BlockSpec((1, *block_pattern.shape[1:]), lambda h: (h, 0, 0)),
        ],
        out_specs=[pl.BlockSpec((1, *shape), lambda h: (h, 0, 0)) for shape in out_shapes],
        out_shape=[
            jax.ShapeDtypeStruct((heads, *shape), kind) for shape, kind in zip(out_shapes, out_types)
        ],
    )(info, values, block_pattern)


def widen_queries(queries, bias_rows):
    scaled = (queries.astype(jnp.float32) * (LANES**-0.5 * LOG2E)).astype(jnp.bfloat16)
    rows = queries.shape[0] // len(bias_rows)
    bias = [jnp.broadcast_to(row, (rows, LANES)).astype(jnp.bfloat16) for row in bias_rows]
    return jnp.concatenate([scaled, jnp.concatenate(bias, 0)], 1)


def split_three(value):
    high = value.astype(jnp.bfloat16).astype(jnp.float32)
    rest = value - high
    middle = rest.astype(jnp.bfloat16).astype(jnp.float32)
    low = rest - middle
    return jnp.concatenate([high, middle, low, jnp.zeros_like(low)], 0)


def peak_eight(scores):
    return jnp.max(scores.reshape(scores.shape[0] // 8, 8, scores.shape[1]), 0)


def finish_rows(numerator, peak):
    total = jnp.maximum(numerator[LANES : LANES + 1], 1e-30)
    normal = (numerator[:LANES] * (1.0 / total)).astype(jnp.bfloat16)
    return normal, split_three(peak + jnp.log2(total))


def far_body(info_ref, *refs, places, tile, step, first_block):
    sources = 2
    query_refs, refs = refs[:places], refs[places:]
    key_refs, value_refs, bias_refs, out_refs, joined_ref, refs = (
        refs[:2],
        refs[2:4],
        refs[4:6],
        refs[6:8],
        refs[8],
        refs[9:],
    )
    (
        held_queries,
        held_bias,
        held_keys,
        held_values,
        marks,
        held_out,
        score_a,
        score_b,
        query_sems,
        key_sems,
        value_sems,
        out_sems,
    ) = refs
    heads, _, tokens = value_refs[0].shape
    jobs = [helper_job(info_ref, number) for number in range(sources)]
    rows = query_refs[0].shape[0]
    tiles = sources * rows // tile
    per_tile = tile // BLOCK
    per_source = rows // tile
    scores = (score_a, score_b)

    def query_copy(source, place):
        target = held_queries.at[source * rows : (source + 1) * rows, :]
        return pltpu.make_async_copy(query_refs[place], target, query_sems.at[source])

    def key_copy(source, head, owner):
        lanes = pl.ds(pl.multiple_of(head * LANES, LANES), LANES)
        return pltpu.make_async_copy(
            key_refs[owner].at[:, lanes], held_keys.at[source, head], key_sems.at[source, head]
        )

    def value_copy(source, head, owner):
        return pltpu.make_async_copy(
            value_refs[owner].at[head], held_values.at[source, head], value_sems.at[source, head]
        )

    def start_head(head):
        for source, (_, _, _, odd) in enumerate(jobs):
            for owner in range(2):

                @pl.when(odd == owner)
                def _(source=source, owner=owner):
                    key_copy(source, head, owner).start()
                    value_copy(source, head, owner).start()

    for source, (hops, _, _, _) in enumerate(jobs):
        for place in range(places):
            pl.when(jnp.minimum(hops, places - 1) == place)(query_copy(source, place).start)
    start_head(0)
    mark_blocks(marks)
    for source in range(sources):
        count = rows // BLOCK
        held_bias[:, source * count : (source + 1) * count, :] = bias_refs[source][
            :, first_block : first_block + count, :
        ]

    def load_queries(place, head):
        lanes = pl.ds(pl.multiple_of(head * LANES, LANES), LANES)
        block = held_queries[pl.ds(pl.multiple_of(place * tile, tile), tile), lanes]
        bias = [held_bias[head, pl.ds(place * per_tile + j, 1), :] for j in range(per_tile)]
        return widen_queries(block, bias)

    def score_step(queries, source, head, first, target):
        spot = slice(first, first + step)
        keys = jnp.concatenate([held_keys[source, head, spot, :], marks[spot, :]], 1)
        part = lax.dot_general(keys, queries, NT, preferred_element_type=jnp.float32)
        target[spot, :] = part
        return peak_eight(part)

    starts = range(0, tokens, step)

    def one_item(head, place, next_head, next_place, current, upcoming, peaks):
        source, next_source = place // per_source, next_place // per_source
        queries = load_queries(next_place, next_head)
        peak = jnp.maximum(jnp.max(peaks, 0, keepdims=True), LEAST_PEAK)
        peaks = numerator = None
        for first in starts:
            found = score_step(queries, next_source, next_head, first, upcoming)
            peaks = found if peaks is None else jnp.maximum(peaks, found)
            weights = jnp.exp2(current[first : first + step, :] - peak).astype(jnp.bfloat16)
            part = jnp.dot(
                held_values[source, head, :, first : first + step], weights, preferred_element_type=jnp.float32
            )
            numerator = part if numerator is None else numerator + part
        normal, three = finish_rows(numerator, peak)
        columns = pl.ds(pl.multiple_of(place * tile, tile), tile)
        held_out[head, :LANES, columns] = normal
        three = jnp.concatenate([three] * (STAT_ROWS // 4), 0).astype(jnp.bfloat16)
        held_out[head, LANES:, columns] = three
        return peaks

    pairs = tiles // 2

    def one_pair(number, peaks):
        head, place = number // pairs, number % pairs * 2
        peaks = one_item(head, place, head, place + 1, score_a, score_b, peaks)
        is_last = place + 2 == tiles
        next_head = jnp.where(is_last, jnp.minimum(head + 1, heads - 1), head)
        next_place = jnp.where(is_last, 0, place + 2)

        @pl.when(next_head != head)
        def _():
            for source in range(sources):
                key_copy(source, next_head, 0).wait()
                value_copy(source, next_head, 0).wait()

        return one_item(head, place + 1, next_head, next_place, score_b, score_a, peaks)

    query_copy(0, 0).wait()
    key_copy(0, 0, 0).wait()
    queries = load_queries(0, 0)
    peaks = None
    for first in starts:
        found = score_step(queries, 0, 0, first, score_a)
        peaks = found if peaks is None else jnp.maximum(peaks, found)
    query_copy(1, 0).wait()
    key_copy(1, 0, 0).wait()
    for source in range(sources):
        value_copy(source, 0, 0).wait()
    for head in range(1, heads):
        start_head(head)
    lax.fori_loop(0, heads * pairs, one_pair, peaks)
    copies = []
    last = places - 1

    def send_out(first, count, columns, target, number):
        copies.append(
            pltpu.make_async_copy(
                held_out.at[first, :count, columns],
                target.at[first * LANES : first * LANES + count, :],
                out_sems.at[number, first],
            )
        )
        copies[-1].start()

    both = [slice(source * rows, (source + 1) * rows) for source in range(sources)]
    for source, columns in enumerate(both):
        stats = [held_out[head, LANES : LANES + 4, columns] for head in range(heads)]
        if 4 * heads < STAT_ROWS:
            stats.append(jnp.zeros((STAT_ROWS - 4 * heads, rows), jnp.bfloat16))
        held_out[heads, :STAT_ROWS, columns] = jnp.concatenate(stats, 0)
        for head in range(heads + 1):
            send_out(head, LANES if head < heads else STAT_ROWS, columns, out_refs[source], source)
    joined = slice(sources * rows, (sources + 1) * rows)
    stats = []
    for head in range(heads):
        pieces = []
        for (hops, _, _, _), columns in zip(jobs, both):
            three = held_out[head, LANES : LANES + 3, columns].astype(jnp.float32)
            stat = jnp.sum(three, 0, keepdims=True)
            pieces.append((held_out[head, :LANES, columns], jnp.where(hops == last, stat, NEG_FILL)))
        held_out[head, :LANES, joined], stat = merge_many(pieces)
        stats.append(split_three(stat))
        send_out(head, LANES, joined, joined_ref, sources)
    if 4 * heads < STAT_ROWS:
        stats.append(jnp.zeros((STAT_ROWS - 4 * heads, rows), jnp.float32))
    held_out[heads, :STAT_ROWS, joined] = jnp.concatenate(stats, 0).astype(jnp.bfloat16)
    send_out(heads, STAT_ROWS, joined, joined_ref, sources)
    for copy in copies:
        copy.wait()


def attend_far(info, queries, keys, turned_values, biases, first_block):
    sources = 2
    heads, deep, tokens = turned_values[0].shape
    rows, width = queries[0].shape
    tile = min(256, rows)
    assert rows // tile * sources % 2 == 0 and rows % tile == 0
    anywhere, in_vmem = pl.BlockSpec(memory_space=pl.ANY), pl.BlockSpec(memory_space=pltpu.VMEM)
    return kernel_call(
        functools.partial(
            far_body, places=len(queries), tile=tile, step=min(512, tokens), first_block=first_block
        ),
        "attend_far",
        16,
        in_specs=[pl.BlockSpec(memory_space=pltpu.SMEM)]
        + [anywhere] * (len(queries) + 2 * sources)
        + [in_vmem] * sources,
        out_specs=[anywhere] * (sources + 1),
        out_shape=[jax.ShapeDtypeStruct((heads * LANES + STAT_ROWS, rows), jnp.bfloat16)] * (sources + 1),
        scratch_shapes=[
            pltpu.VMEM((sources * rows, width), jnp.bfloat16),
            pltpu.VMEM((heads, sources * rows // BLOCK, LANES), jnp.float32),
            pltpu.VMEM((sources, heads, tokens, LANES), jnp.bfloat16),
            pltpu.VMEM((sources, heads, deep, tokens), jnp.bfloat16),
            pltpu.VMEM((tokens, LANES), jnp.bfloat16),
            pltpu.VMEM((heads + 1, LANES + STAT_ROWS, (sources + 1) * rows), jnp.bfloat16),
            pltpu.VMEM((tokens, tile), jnp.float32),
            pltpu.VMEM((tokens, tile), jnp.float32),
            pltpu.SemaphoreType.DMA((sources,)),
            pltpu.SemaphoreType.DMA((sources, heads)),
            pltpu.SemaphoreType.DMA((sources, heads)),
            pltpu.SemaphoreType.DMA((sources + 1, heads + 1)),
        ],
    )(info, *queries, *keys, *turned_values, *biases)


def local_body(query_ref, key_ref, value_ref, bias_ref, out_ref, stat_ref, marks, score_a, score_b, *, tile, spots):
    tokens = key_ref.shape[0]
    tiles = tokens // tile
    per_tile = tile // BLOCK
    scores = (score_a, score_b)
    key_place = lax.broadcasted_iota(jnp.int32, (tile, tile), 0)
    query_place = lax.broadcasted_iota(jnp.int32, (tile, tile), 1)
    mark_blocks(marks)
    hidden = (key_place // BLOCK == query_place // BLOCK) & (key_place > query_place)

    def load_queries(place):
        rows = [bias_ref[0, place * per_tile + j : place * per_tile + j + 1, :] for j in range(per_tile)]
        return widen_queries(query_ref[place * tile : (place + 1) * tile, :], rows)

    def score_step(queries, place, number, target):
        spot = slice(number * tile, (number + 1) * tile)
        keys = jnp.concatenate([key_ref[spot, :], marks[spot, :]], 1)
        part = lax.dot_general(keys, queries, NT, preferred_element_type=jnp.float32)
        if number == place:
            part = jnp.where(hidden, NEG_FILL, part)
        target[number * tile : (number + 1) * tile, :] = part
        return peak_eight(part)

    peaks = score_step(load_queries(0), 0, 0, scores[0])
    for place in range(tiles):
        current, upcoming = scores[place % 2], scores[(place + 1) % 2]
        more = place + 1 < tiles
        queries = load_queries(place + 1) if more else None
        peak = jnp.max(peaks, 0, keepdims=True)
        peaks = numerator = None
        for number in range(place + 2):
            if more:
                found = score_step(queries, place + 1, number, upcoming)
                peaks = found if peaks is None else jnp.maximum(peaks, found)
            if number <= place:
                spot = slice(number * tile, (number + 1) * tile)
                weights = jnp.exp2(current[spot, :] - peak).astype(jnp.bfloat16)
                part = jnp.dot(value_ref[0, :, spot], weights, preferred_element_type=jnp.float32)
                numerator = part if numerator is None else numerator + part
        normal, stats = finish_rows(numerator, peak)
        stats = jnp.concatenate([stats] * (STAT_ROWS // 4), 0).astype(jnp.bfloat16)
        for j in range(per_tile):
            columns = pl.ds(spots[place * per_tile + j] * BLOCK, BLOCK)
            out_ref[:, columns] = normal[:, j * BLOCK : (j + 1) * BLOCK]
            stat_ref[0, :, columns] = stats[:, j * BLOCK : (j + 1) * BLOCK]


def attend_local(queries, keys, turned_values, bias, spots, head, count):
    tokens = keys.shape[0]
    tile = min(256, tokens)
    blocks = bias.shape[1]
    return kernel_call(
        functools.partial(local_body, tile=tile, spots=spots),
        "attend_local",
        10,
        grid=(count,),
        in_specs=[
            pl.BlockSpec((tokens, LANES), lambda h: (0, head + h)),
            pl.BlockSpec((tokens, LANES), lambda h: (0, head + h)),
            pl.BlockSpec((1, LANES + STAT_ROWS, tokens), lambda h: (head + h, 0, 0)),
            pl.BlockSpec((1, blocks, LANES), lambda h: (head + h, 0, 0)),
        ],
        out_specs=[
            pl.BlockSpec((LANES, tokens), lambda h: (h, 0)),
            pl.BlockSpec((1, STAT_ROWS, tokens), lambda h: (h, 0, 0)),
        ],
        out_shape=[
            jax.ShapeDtypeStruct((count * LANES, tokens), jnp.bfloat16),
            jax.ShapeDtypeStruct((count, STAT_ROWS, tokens), jnp.bfloat16),
        ],
        scratch_shapes=[pltpu.VMEM((tokens, LANES), jnp.bfloat16)]
        + [pltpu.VMEM((tokens, tile), jnp.float32)] * 2,
    )(queries, keys, turned_values, bias)


def packed_stats(ref, heads):
    first = heads * LANES
    return [
        sum(ref[p : p + 1, :].astype(jnp.float32) for p in range(first + 4 * head, first + 4 * head + 3))
        for head in range(heads)
    ]


def merge_many(pieces):
    peak = functools.reduce(jnp.maximum, [stat for _, stat in pieces])
    parts = [jnp.exp2(stat - peak) for _, stat in pieces]
    total = sum(parts)
    mixed = sum(piece.astype(jnp.float32) * (part / total) for (piece, _), part in zip(pieces, parts))
    return mixed.astype(jnp.bfloat16), peak + jnp.log2(total)


def merge_flags(info_ref, hops):
    own = [helper_job(info_ref, number)[0] == hops for number in range(2)]
    return [info_ref[0] >= 2, *own]


def merge_far_body(info_ref, *refs, heads, hops):
    piece_refs, out_ref = refs[:-1], refs[-1]
    flags = merge_flags(info_ref, hops)
    piece_stats = [packed_stats(ref, heads) for ref in piece_refs]
    stats = []
    for head in range(heads):
        rows = slice(head * LANES, (head + 1) * LANES)
        pieces = [
            (ref[rows, :], jnp.where(flag, stat[head], NEG_FILL))
            for ref, stat, flag in zip(piece_refs, piece_stats, flags)
        ]
        out_ref[rows, :], stat = merge_many(pieces)
        stats.append(split_three(stat))
    if 4 * heads < STAT_ROWS:
        stats.append(jnp.zeros((STAT_ROWS - 4 * heads, out_ref.shape[1]), jnp.float32))
    out_ref[heads * LANES :, :] = jnp.concatenate(stats, 0).astype(jnp.bfloat16)


def merge_far(info, pieces, heads, hops):
    in_vmem = pl.BlockSpec(memory_space=pltpu.VMEM)
    return kernel_call(
        functools.partial(merge_far_body, heads=heads, hops=hops),
        "merge_far",
        40,
        in_specs=[pl.BlockSpec(memory_space=pltpu.SMEM)] + [in_vmem] * len(pieces),
        out_specs=in_vmem,
        out_shape=jax.ShapeDtypeStruct(pieces[0].shape, jnp.bfloat16),
    )(info, *pieces)


def merge_local_body(info_ref, *refs, heads, runs, stages, groups):
    local_refs, held_refs = refs[: 2 * runs], refs[2 * runs : -1 - groups]
    out_refs, turned_ref = refs[-1 - groups : -1], refs[-1]
    owners = [
        (run, spot) for run in range(runs) for spot in range(local_refs[2 * run].shape[0] // LANES)
    ]
    others = len(held_refs) // stages
    wide = out_refs[0].shape[0] // stages
    flags = merge_flags(info_ref, 0)
    for stage in range(stages):
        lanes = slice(stage * groups * wide, (stage + 1) * groups * wide)
        here = held_refs[stage * others : (stage + 1) * others]
        far_stats = [packed_stats(ref, heads) for ref in here]
        for head in range(heads):
            rows = slice(head * LANES, (head + 1) * LANES)
            run, spot = owners[head]
            normal_ref, stat_ref = local_refs[2 * run : 2 * run + 2]
            stat = sum(stat_ref[spot, p : p + 1, lanes].astype(jnp.float32) for p in range(3))
            pieces = [(normal_ref[spot * LANES : (spot + 1) * LANES, lanes], stat)]
            pieces += [
                (ref[rows, :], jnp.where(flag, far_stat[head], NEG_FILL))
                for ref, far_stat, flag in zip(here, far_stats, flags)
            ]
            turned_ref[:, rows] = merge_many(pieces)[0].T
        for place, out_ref in enumerate(out_refs):
            apart = jnp.where(info_ref[0] & 1 == 1, bit_reverse(place, groups.bit_length() - 1), place)
            first = pl.multiple_of((info_ref[1] ^ apart) * wide, wide)
            out_ref[stage * wide : (stage + 1) * wide, :] = turned_ref[pl.ds(first, wide), :]


def merge_local(info, local, first, stages, chunks, pieces, heads, groups):
    columns = local[0][0].shape[1] // chunks * stages
    assert first % stages == 0
    specs = [pl.BlockSpec(memory_space=pltpu.SMEM)]
    for normal, stat in local:
        specs += [
            pl.BlockSpec((normal.shape[0], columns), lambda i: (0, first // stages)),
            pl.BlockSpec((*stat.shape[:2], columns), lambda i: (0, 0, first // stages)),
        ]
    specs += [pl.BlockSpec(piece.shape, lambda i: (0, 0)) for piece in pieces]
    return kernel_call(
        functools.partial(
            merge_local_body, heads=heads, runs=len(local), stages=stages, groups=groups
        ),
        "merge_local",
        40,
        grid=(1,),
        in_specs=specs,
        out_specs=[pl.BlockSpec((columns // groups, heads * LANES), lambda i: (0, 0))] * groups,
        out_shape=[jax.ShapeDtypeStruct((columns // groups, heads * LANES), jnp.bfloat16)] * groups,
        scratch_shapes=[pltpu.VMEM((columns // stages, heads * LANES), jnp.bfloat16)],
    )(info, *[array for both in local for array in both], *pieces)


def bit_reverse(place, bits):
    return sum((place >> bit & 1) << (bits - 1 - bit) for bit in range(bits))


def project_body(info_ref, weight_ref, *refs, sources, stages, cuts):
    bits = sources.bit_length() - 1
    own_refs, other_refs = refs[: sources - 1], refs[sources - 1 : 2 * sources - 2]
    part_refs = refs[2 * sources - 2 : 2 * sources - 2 + stages * sources]
    out_ref, held, outs, sems, out_sems = refs[-5:]
    depth, columns = weight_ref.shape
    half = depth // 2
    width = columns // cuts
    parity = info_ref[0] & 1
    copies = []
    for cut in range(cuts):
        lanes = slice(cut * width, (cut + 1) * width)
        pairs = [(weight_ref.at[:, lanes], held.at[cut, :depth, :])]
        for place in range(1, sources):
            own = pl.multiple_of(place * depth + parity * half, half)
            other = pl.multiple_of(bit_reverse(place, bits) * depth + (1 - parity) * half, half)
            pairs.append((own_refs[place - 1].at[:, lanes], held.at[cut, pl.ds(own, half), :]))
            pairs.append((other_refs[place - 1].at[:, lanes], held.at[cut, pl.ds(other, half), :]))
        copies.append(
            [
                pltpu.make_async_copy(origin, target, sems.at[cut, number])
                for number, (origin, target) in enumerate(pairs)
            ]
        )
        for copy in copies[-1]:
            copy.start()
    rows = [
        jnp.concatenate([part_refs[stage * sources + place][...] for place in range(sources)], 1)
        for stage in range(stages)
    ]
    left = jnp.concatenate(rows, 0)
    out_copies = []
    for cut in range(cuts):
        for copy in copies[cut]:
            copy.wait()
        outs[cut] = jnp.dot(left, held[cut], preferred_element_type=jnp.float32).astype(jnp.bfloat16)
        out_copies.append(
            pltpu.make_async_copy(
                outs.at[cut], out_ref.at[:, cut * width : (cut + 1) * width], out_sems.at[cut]
            )
        )
        out_copies[-1].start()
    for copy in out_copies:
        copy.wait()


def project(info, weight_rows, own, other, parts):
    sources, stages, cuts = len(parts[0]), len(parts), 4
    depth, columns = weight_rows.shape
    rows = sum(row[0].shape[0] for row in parts)
    anywhere, in_vmem = pl.BlockSpec(memory_space=pl.ANY), pl.BlockSpec(memory_space=pltpu.VMEM)
    flat = [piece for row in parts for piece in row]
    return kernel_call(
        functools.partial(project_body, sources=sources, stages=stages, cuts=cuts),
        "project",
        15,
        in_specs=[pl.BlockSpec(memory_space=pltpu.SMEM)]
        + [anywhere] * (2 * sources - 1)
        + [in_vmem] * len(flat),
        out_specs=anywhere,
        out_shape=jax.ShapeDtypeStruct((rows, columns), jnp.bfloat16),
        scratch_shapes=[
            pltpu.VMEM((cuts, sources * depth, columns // cuts), jnp.bfloat16),
            pltpu.VMEM((cuts, rows, columns // cuts), jnp.bfloat16),
            pltpu.SemaphoreType.DMA((cuts, 2 * sources - 1)),
            pltpu.SemaphoreType.DMA((cuts,)),
        ],
    )(info, weight_rows, *own, *other, *flat)


def shift(value, steps, first, last):
    return lax.ppermute(value, "ctx", [(source, source + steps) for source in range(first, last)])


def swap_sibling(value):
    return lax.ppermute(value, "ctx", [(i, i ^ 1) for i in range(lax.axis_size("ctx"))])


def swap_head(value, even_bits, odd_bits):
    count = lax.axis_size("head")
    pairs = []
    for place in range(lax.axis_size("ctx")):
        bits = odd_bits if place % 2 else even_bits
        pairs += [(place * count + i, place * count + (i ^ bits)) for i in range(count)]
    return lax.ppermute(value, ("ctx", "head"), pairs)


def start_weights(weight_rows, parity, *earlier):
    half = weight_rows.shape[0] // 2
    return [lax.dynamic_slice_in_dim(after(weight_rows, *earlier), parity * half, half, 0)]


def double_weights(held, *earlier):
    bits = lax.axis_size("head").bit_length() - 1
    number = len(held).bit_length() - 1
    sent = [after(piece, *earlier) for piece in held]
    return held + [swap_head(piece, 1 << number, 1 << (bits - 1 - number)) for piece in sent]


def after(value, *earlier):
    return lax.optimization_barrier((value, *earlier))[0]


def chunk_of(array, axis, number, groups, chunks):
    shape = array.shape
    count = shape[axis] // (groups * chunks)
    split = array.reshape(shape[:axis] + (groups, chunks, count) + shape[axis + 1 :])
    piece = lax.index_in_dim(split, number, axis + 1, False)
    return piece.reshape(shape[:axis] + (groups * count,) + shape[axis + 1 :])


def per_device(query_states, key_states, value_states, block_pattern, helper_distances, out_weight):
    count = lax.axis_size("ctx")
    groups = lax.axis_size("head")
    me = lax.axis_index("ctx")
    group = lax.axis_index("head")
    tokens, heads, head_dim = query_states.shape
    blocks = tokens // BLOCK
    chunks = min(4, blocks // groups)
    per_piece = blocks // groups // chunks
    width = heads * head_dim
    parity = me & 1
    bits = groups.bit_length() - 1
    turns = [(place, bit_reverse(place, bits)) for place in range(groups)]
    weight_rows = out_weight.reshape(width, out_weight.shape[2])
    spots = []
    for block in range(blocks):
        part, rest = divmod(block, chunks * per_piece)
        spots.append((rest // per_piece * groups + part) * per_piece + rest % per_piece)

    def flat(array):
        return array.reshape(array.shape[0], width)

    def query_chunk(number):
        return flat(lax.optimization_barrier(chunk_of(query_states, 0, number, groups, chunks)))

    def exchange(pieces):
        return [pieces[0]] + [swap_head(pieces[place], *turns[place]) for place in range(1, groups)]

    places = count // 4
    info = jnp.concatenate([jnp.stack([me, group]), helper_distances])
    hops = [[query_chunk(number)] for number in range(chunks)]

    def move_down(number, *earlier):
        done = len(hops[number])
        moving = after(hops[number][-1], *earlier)
        hops[number].append(shift(moving, -2, 2, count - 2 * (done - 1)))

    for number in range(min(2, chunks)):
        move_down(number)
    keys = flat(key_states)
    turned_values, local_bias, *biases = prepare(info, flat(value_states), block_pattern, spots)
    both_keys = [keys, swap_sibling(keys)]
    both_values = [turned_values, swap_sibling(turned_values)]
    queries = flat(query_states)
    early = heads - max(1, heads // 4)
    for _ in range(1, places):
        move_down(0)
    local = [attend_local(queries, keys, turned_values, local_bias, spots, 0, early)]
    queries = after(queries, local[0][0], hops[0][-1])
    local.append(attend_local(queries, keys, turned_values, local_bias, spots, early, heads - early))
    for number in range(2, chunks):
        move_down(number, local[number % 2][0])

    def attend(number, *earlier):
        arrays = [*hops[number][:-1], after(hops[number][-1], *earlier)]
        return attend_far(info, arrays, both_keys, both_values, biases, number * groups * per_piece)

    def move_up(piece, hops_left):
        return shift(piece, 2, 0, count - 2 * hops_left)

    def finish(first, stages, *earlier):
        pieces = [piece for number in range(first, first + stages) for piece in (moved[number], *own[number])]
        pieces[0] = after(pieces[0], *earlier)
        merged = merge_local(info, local, first, stages, chunks, pieces, heads, groups)
        return merged[0], exchange(merged)

    own, moved, parts = {}, {}, []
    last = local[1][0]
    held = double_weights(start_weights(weight_rows, parity, hops[0][1]))
    waits = {0: held[1:]}
    while len(held) < groups:
        first = len(held)
        held = double_weights(held)
        waits[1], waits[3] = waits.get(1, []) + held[first : first + 1], held[first + 1 :]
    other = [swap_sibling(piece) for piece in held[1:]]
    for slot in range(chunks + places - 1):
        for number in [1, 2] if slot == 0 else [slot + 2]:
            for _ in range(1, places if number < chunks else 1):
                move_down(number, last)
        if slot < chunks:
            arrived = waits.get(slot, [])
            *own[slot], last = attend(slot, last, *arrived)
            moved[slot] = move_up(last, places)
        for behind in range(1, places):
            number = slot - behind
            if 0 <= number < chunks:
                waited = [moved[number - 1]] if 0 < number < chunks - 1 else []
                pieces = [after(moved[number], last, *waited), *own[number]]
                last = merge_far(info, pieces, heads, places - behind)
                moved[number] = move_up(last, places - behind)
                if number == chunks - 2 and chunks == 4 and places == 2:
                    last, exchanged = finish(0, 2, last)
                    parts.append(exchanged)
    done = sum(row[0].shape[0] for row in parts) * chunks * groups // tokens
    for number in range(done, chunks):
        waited = other if number == done else []
        if number == chunks - 1:
            waited = [*waited, *(piece for row in parts for piece in row)]
        last, exchanged = finish(number, 1, last, *waited)
        parts.append(exchanged)
    return project(info, weight_rows, held[1:], other, parts)


def solution(mesh):
    placed = (
        P("ctx", "head", None),
        P("ctx", "head", None),
        P("ctx", "head", None),
        P("head", None, None),
        P(),
        P("head", None, None),
    )
    return jax.shard_map(
        per_device, mesh=mesh, in_specs=placed, out_specs=P(("ctx", "head"), None), check_vma=False
    )
```
